128 devices in a mesh: dp: 2 (over y_lo), expert: 64 (over x, z, y_hi, core).
Axes of the slice: x: 4, y: 4 (y_hi: 2, y_lo: 2; y = y_hi * 2 + y_lo), z: 4, core: 2. Of those that a mesh axis runs over, the one named last changes fastest.
Arguments:
- tokens: bfloat16 [32768, 1024], P(('dp', 'expert')), may hold values from -6 to 6
- segment_ids: int32 [128, 256], P(('dp', 'expert')), may hold values from 0 to 7, never falling along the last dimension, each value on 1 to 64 neighbouring positions
- padding: int32 [128, 256], P(('dp', 'expert')), may hold values 0 or 1
- expert_ids: int32 [32768], P(('dp', 'expert')), may hold values from 0 to 63, as said below
- slots: int32 [32768], P(('dp', 'expert')), may hold values from 0 to 5, as said below
- norm1_gain: float32 [1024], replicated, may hold values from 0.5 to 1.5
- norm1_bias: float32 [1024], replicated, may hold values from -1 to 1
- qkv_weight: bfloat16 [1024, 3072], replicated, may hold values from -0.1875 to 0.1875
- out_weight: bfloat16 [1024, 1024], replicated, may hold values from -0.75 to 0.75
- norm2_gain: float32 [1024], replicated, may hold values from 0.5 to 1.5
- norm2_bias: float32 [1024], replicated, may hold values from -1 to 1
- up_weight: bfloat16 [64, 1024, 4096], P('expert'), may hold values from -0.1875 to 0.1875
- down_weight: bfloat16 [64, 4096, 1024], P('expert'), may hold values from -0.09375 to 0.09375
- cotangent: bfloat16 [32768, 1024], P(('dp', 'expert')), may hold values from -6 to 6
Outputs:
- output: bfloat16 [32768, 1024], P(('dp', 'expert'))
- input_grad: float32 [32768, 1024], P(('dp', 'expert'))
- norm1_gain_grad: float32 [1024], P(('dp', 'expert'))
- norm1_bias_grad: float32 [1024], P(('dp', 'expert'))
- qkv_weight_grad: float32 [1024, 3072], P(('dp', 'expert'))
- out_weight_grad: float32 [1024, 1024], P(('dp', 'expert'))
- norm2_gain_grad: float32 [1024], P(('dp', 'expert'))
- norm2_bias_grad: float32 [1024], P(('dp', 'expert'))
- up_weight_grad: float32 [64, 1024, 4096], P('expert', 'dp')
- down_weight_grad: float32 [64, 4096, 1024], P('expert', 'dp')
The draws below stay inside these ranges and needn't reach their ends.
Inputs may be any that keep to these rules, and one draw needn't show every extreme that they name: `expert_ids`: the tokens of one device name each expert at most 6 times; in every draw one expert is named exactly 6 times by the tokens of every device. Tokens of one device that name the same expert have different slots.
All inputs are finite; a program needn't handle non-finite values. No bound on the sum of `padding` on one device may be relied on, other than what follows from the above.
Results may differ from the reference program's by a relative error of at most 0.011.
Values may be sent and summed in bfloat16 or wider, within the bound.
No kernel may reach another device: no remote copies, remote signals or barrier semaphores. Data moves between devices by JAX's collectives and lax.ppermute only.
A program may use at most 192 MiB of HBM per device.

```python
import math
import jax
import jax.numpy as jnp
import numpy as np
from jax import lax

D = 1024
HEADS = 16
HEAD_DIM = 64
FF = 4096
TOK_DEV = 256
EXPERTS = 64
CAP = 6
ROWS = 128
TOKENS = 32768
N_DP = 2
N_EXPERT = 64


def route_places(key):
    first_key, device_key = jax.random.split(jax.random.fold_in(key, 17))
    favored = jax.random.randint(first_key, (), 0, EXPERTS)
    total_slots = EXPERTS * CAP
    owners = jnp.arange(total_slots, dtype=jnp.int32) // CAP

    def one_device(sub_key):
        rank_key, order_key = jax.random.split(sub_key)
        ranking = jax.random.permutation(rank_key, total_slots).astype(jnp.int32)
        scoring = ranking + jnp.where(owners == favored, 0, total_slots).astype(jnp.int32)
        picked = jnp.argsort(scoring)[:TOK_DEV].astype(jnp.int32)
        return jax.random.permutation(order_key, picked)
    places = jax.vmap(one_device)(jax.random.split(device_key, TOKENS // TOK_DEV))
    return places.reshape(TOKENS).astype(jnp.int32)


def draw_expert_ids(key, part):
    places = route_places(key)
    return (places // CAP).astype(jnp.int32)


def draw_slots(key, part):
    places = route_places(key)
    return (places % CAP).astype(jnp.int32)


def plant(values, key, low, top_value):
    extent = values.shape
    index_at = [jax.random.randint(jax.random.fold_in(key, axis), (), 0, extent[axis]) for axis in range(len(extent))]
    values = values.at[tuple(index_at)].set(low)
    longest = extent.index(max(extent))
    index_at[longest] = (index_at[longest] + 1) % extent[longest]
    return values.at[tuple(index_at)].set(top_value)


def block_scale(rng, extent, pieces, least, high):
    level, own = 1.0, jax.random.fold_in(rng, 6)
    for dim, blocks in pieces:
        heights = jnp.exp(jax.random.uniform(jax.random.fold_in(own, dim), (blocks,), jnp.float32, least / len(pieces), high / len(pieces)))
        level = level * jnp.repeat(heights, extent[dim] // blocks).reshape([-1 if axis == dim else 1 for axis in range(len(extent))])
    return level


def length_profile(number_of, total, bound, skew):
    portions = [(1 << 20) // math.isqrt(standing ** skew) + 1 for standing in range(2, number_of + 1)]
    rest, counts = total - bound - (number_of - 1), [1] * (number_of - 1)
    while rest > 0:
        candidates = [i for i in range(number_of - 1) if counts[i] < bound]
        whole, left = sum([portions[i] for i in candidates]), rest
        for i in candidates:
            addition = min(bound - counts[i], max(1, left * portions[i] // whole), rest)
            counts[i] = counts[i] + addition
            rest = rest - addition
    return np.array([bound] + counts)


def uneven(own_key, amount, total, reach, lean):
    if amount == 2:
        one = jax.random.randint(own_key, (), max(1, total - reach), min(reach, total - 1) + 1)
        return jnp.stack([one, total - one])
    lengths = jnp.asarray(length_profile(amount, total, reach, lean), jnp.int32)
    pairs = (amount - 1) // 2
    donor, sink = lengths[1:1 + 2 * pairs:2], lengths[2:2 + 2 * pairs:2]
    slack = jnp.minimum(donor - 1, reach - sink)
    shifted = jax.random.randint(jax.random.fold_in(own_key, 1), (pairs,), 0, 1 << 20) % (slack + 1)
    lengths = lengths.at[1:1 + 2 * pairs:2].set(donor - shifted).at[2:2 + 2 * pairs:2].set(sink + shifted)
    return lengths[jax.random.permutation(jax.random.fold_in(own_key, 2), amount)]


def bell_draw(stream_key, extent, deviation, bound, shards=(), kind=jnp.bfloat16):
    values = jax.random.normal(stream_key, extent, jnp.float32) * deviation
    if len(shards) > 0:
        values = block_scale(stream_key, extent, shards, -0.22, 0.18) * values
    return jnp.clip(values, min=-bound, max=bound).astype(kind)


def setup_inputs(seed: int = 0) -> dict:
    keys = jax.random.split(jax.random.key(seed), 15)
    return {
        "tokens": bell_draw(keys[0], (TOKENS, D), 1.0, 6.0, ((0, 128),)),
        "segment_ids": jax.vmap(lambda own: jnp.searchsorted(jnp.cumsum(uneven(own, 8, TOK_DEV, TOK_DEV // 4, 1)), jnp.arange(TOK_DEV), side="right"))(jax.random.split(keys[1], ROWS)).reshape((ROWS, TOK_DEV)).astype(jnp.int32),
        "padding": plant((jax.random.randint(keys[2], (ROWS, TOK_DEV), 0, 8) < 7).astype(jnp.int32), jax.random.fold_in(keys[2], 1), 0, 1),
        "expert_ids": draw_expert_ids(jax.random.fold_in(keys[14], 71), 0),
        "slots": draw_slots(jax.random.fold_in(keys[14], 71), 0),
        "norm1_gain": jnp.clip(1.0 + 0.1 * jax.random.normal(keys[5], (D,), jnp.float32), 0.5, 1.5),
        "norm1_bias": bell_draw(keys[6], (D,), 0.2, 1.0, (), jnp.float32),
        "qkv_weight": bell_draw(keys[7], (D, 3 * D), D ** -0.5, 0.1875),
        "out_weight": bell_draw(keys[8], (D, D), (D // 16) ** -0.5, 0.75),
        "norm2_gain": jnp.clip(1.0 + 0.1 * jax.random.normal(keys[9], (D,), jnp.float32), 0.5, 1.5),
        "norm2_bias": bell_draw(keys[10], (D,), 0.2, 1.0, (), jnp.float32),
        "up_weight": bell_draw(keys[11], (EXPERTS, D, FF), D ** -0.5, 0.1875, ((0, 64),)),
        "down_weight": bell_draw(keys[12], (EXPERTS, FF, D), FF ** -0.5, 0.09375, ((0, 64),)),
        "cotangent": bell_draw(keys[13], (TOKENS, D), 1.0, 6.0, ((0, 128),)),
    }


@jax.custom_vjp
def low(v):
    return lax.optimization_barrier(v.astype(jnp.bfloat16)).astype(jnp.float32)

@jax.custom_vjp
def low_back(v):
    return v

def low_keep(v):
    return (low(v), None)

def low_pass(kept, grad):
    return (grad,)

def back_keep(v):
    return (v, None)

def back_low(kept, grad):
    return (low(grad),)
low.defvjp(low_keep, low_pass)
low_back.defvjp(back_keep, back_low)

def layer_norm(values, gain, bias):
    center = values - lax.optimization_barrier(jnp.mean(values, -1, keepdims=True))
    spread = lax.optimization_barrier(jnp.mean(center * center, -1, keepdims=True))
    return center * lax.rsqrt(spread + 1e-05) * gain + bias

def attend_rows(packed):
    qkv_rows, segment_rows, padding_rows = packed
    groups = segment_rows.shape[0]
    length = segment_rows.shape[1]
    queries = qkv_rows[..., :D].reshape(groups, length, HEADS, HEAD_DIM)
    keys_all = qkv_rows[..., D:2 * D].reshape(groups, length, HEADS, HEAD_DIM)
    values_all = qkv_rows[..., 2 * D:].reshape(groups, length, HEADS, HEAD_DIM)
    scores = jnp.einsum('gqhe,gkhe->ghqk', queries, keys_all, precision=lax.Precision.HIGHEST) * HEAD_DIM ** (-0.5)
    scores = low_back(scores)
    position = jnp.arange(length, dtype=jnp.int32)
    same = segment_rows[:, :, None] == segment_rows[:, None, :]
    causal = (position[:, None] >= position[None, :])[None]
    visible = (padding_rows[:, None, :] == 1) | (position[:, None] == position[None, :])[None]
    allowed = same & causal & visible
    masked = jnp.where(allowed[:, None], scores, -1000000000.0)
    peak = lax.optimization_barrier(jnp.max(masked, -1, keepdims=True))
    weights = jnp.exp(masked - peak)
    weights = weights / lax.optimization_barrier(jnp.sum(weights, -1, keepdims=True))
    weights = low(weights)
    mixed = jnp.einsum('ghqk,gkhe->gqhe', weights, values_all, precision=lax.Precision.HIGHEST)
    return mixed.reshape(groups, length, D)

def expert_rows(packed):
    rows_in, up_one, down_one = packed
    hidden = low_back(jnp.einsum('grd,df->grf', rows_in, up_one, precision=lax.Precision.HIGHEST))
    active = low(jax.nn.gelu(hidden))
    result = jnp.einsum('grf,fd->grd', active, down_one, precision=lax.Precision.HIGHEST)
    return low_back(low(result))

def forward(inputs, norm1_gain, norm1_bias, qkv_weight, out_weight, norm2_gain, norm2_bias, up_weight, down_weight, segment_ids, padding, expert_ids, slots):
    normed = low(layer_norm(inputs, norm1_gain, norm1_bias))
    qkv = low_back(low(jnp.dot(normed, qkv_weight, precision=lax.Precision.HIGHEST)))
    group = min(ROWS, max(1, 4096 // TOK_DEV))
    batches = ROWS // group
    shaped = qkv.reshape(batches, group, TOK_DEV, 3 * D)
    mixed = lax.map(jax.checkpoint(attend_rows), (shaped, segment_ids.reshape(batches, group, TOK_DEV), padding.reshape(batches, group, TOK_DEV)))
    mixed = low_back(low(mixed.reshape(TOKENS, D)))
    branch = low_back(jnp.dot(mixed, out_weight, precision=lax.Precision.HIGHEST))
    resid = inputs + branch
    second = low_back(low(layer_norm(resid, norm2_gain, norm2_bias)))
    owner = jnp.arange(TOKENS, dtype=jnp.int32) // TOK_DEV
    dp_group = owner // N_EXPERT
    position = owner % N_EXPERT * CAP + slots
    buffer = jnp.zeros((EXPERTS, N_DP, N_EXPERT * CAP, D), jnp.float32).at[expert_ids, dp_group, position].set(second)
    results = lax.map(jax.checkpoint(expert_rows), (buffer, up_weight, down_weight))
    returned = results[expert_ids, dp_group, position]
    return resid + returned

def reference(tokens, segment_ids, padding, expert_ids, slots, norm1_gain, norm1_bias, qkv_weight, out_weight, norm2_gain, norm2_bias, up_weight, down_weight, cotangent):
    floats = (tokens.astype(jnp.float32), norm1_gain.astype(jnp.float32), norm1_bias.astype(jnp.float32), qkv_weight.astype(jnp.float32), out_weight.astype(jnp.float32), norm2_gain.astype(jnp.float32), norm2_bias.astype(jnp.float32), up_weight.astype(jnp.float32), down_weight.astype(jnp.float32))

    def run(*values_in):
        return forward(*values_in, segment_ids, padding, expert_ids, slots)
    result, pullback = jax.vjp(run, *floats)
    grads = pullback(cotangent.astype(jnp.float32))
    return (result.astype(jnp.bfloat16), grads[0], grads[1], grads[2], grads[3], grads[4], grads[5], grads[6], grads[7], grads[8])
```

```python
import jax
import jax.numpy as jnp
from jax import lax
from jax.sharding import Mesh
from jax.sharding import PartitionSpec as P

HEADS = 16
HEAD_DIM = 64
SPLIT = ("dp", "x", "z", "yh", "core")
PEERS = ("x", "z", "yh", "core")
SIZES = (2, 4, 4, 2, 2)
SWAP = [(0, 1), (1, 0)]
F32 = jnp.float32
BF16 = jnp.bfloat16


def mm(a, b, dims):
    return lax.dot_general(a, b, (dims, ((), ())), preferred_element_type=F32)


def nn(a, b):
    return mm(a, b, ((1,), (0,)))


def nt(a, b):
    return mm(a, b, ((1,), (1,)))


def tn(a, b):
    return mm(a, b, ((0,), (0,)))


def layer_stats(values):
    center = values - jnp.mean(values, -1, keepdims=True)
    spread = jnp.mean(center * center, -1, keepdims=True)
    factor = lax.rsqrt(spread + 1e-05)
    return (center * factor, factor)


def norm_back(grad_out, normal, factor, gain):
    grad_hat = grad_out * gain
    return factor * (
        grad_hat
        - jnp.mean(grad_hat, -1, keepdims=True)
        - normal * jnp.mean(grad_hat * normal, -1, keepdims=True)
    )


def exchange(rows):
    return lax.all_to_all(rows.reshape(64, 8, 1024), PEERS, 0, 0, tiled=True).reshape(512, 1024)


def gelu_pair(v):
    scale = 0.7978845608028654
    square = v * v
    t = jnp.tanh(scale * v * (1.0 + 0.044715 * square))
    half = 0.5 * (1.0 + t)
    slope = half + 0.5 * v * (1.0 - t * t) * scale * (1.0 + 3 * 0.044715 * square)
    return v * half, slope


def swap_half(mine, core):
    width = mine.shape[1] // 2
    keep = lax.dynamic_slice_in_dim(mine, core * width, width, 1)
    send = lax.dynamic_slice_in_dim(mine, (1 - core) * width, width, 1)
    return keep, lax.ppermute(send, "core", SWAP)


def scatter_sum(part, axes):
    names = list(SPLIT)
    first = [names.index(a) for a in axes]
    rest = [i for i in range(5) if i not in first]
    width = part.shape[1]
    shaped = part.reshape(SIZES + (8, width)).transpose(first + rest + [5, 6]).reshape(4, 256, width)
    got = lax.all_to_all(shaped, axes, 0, 0, tiled=True)
    summed = jnp.sum(got.astype(F32), 0).astype(BF16).reshape(32, 8, width)
    got = lax.all_to_all(summed, tuple(names[i] for i in rest), 0, 0, tiled=True)
    total = jnp.sum(got.reshape(16, 2, 8, width).astype(F32), 0)
    return total.transpose(1, 0, 2).reshape(8, 2 * width)


def shards(
    tokens,
    segment_ids,
    padding,
    expert_ids,
    slots,
    norm1_gain,
    norm1_bias,
    qkv_weight,
    out_weight,
    norm2_gain,
    norm2_bias,
    up_weight,
    down_weight,
    cotangent,
):
    length, width = tokens.shape
    score_scale = HEAD_DIM ** (-0.5)
    dp = lax.axis_index("dp")
    core = lax.axis_index("core")
    up = up_weight[0]
    down = down_weight[0]

    slot_index = expert_ids * 8 + slots
    dispatch = (slot_index[:, None] == jnp.arange(512, dtype=jnp.int32)[None, :]).astype(BF16)
    dense = jnp.arange(384, dtype=jnp.int32)
    compact = (
        (dense // 6 * 8 + dense % 6)[:, None] == jnp.arange(512, dtype=jnp.int32)[None, :]
    ).astype(BF16)

    grad_arrived = exchange(tn(dispatch, cotangent).astype(BF16))
    grad_own = nn(compact, grad_arrived).astype(BF16)
    grad_other = lax.ppermute(grad_own, "dp", SWAP)

    inputs = tokens.astype(F32)
    normal1, factor1 = layer_stats(inputs)
    normed = (normal1 * norm1_gain + norm1_bias).astype(BF16)
    normed_other = lax.ppermute(normed, "core", SWAP)
    qkv = nn(normed, qkv_weight).astype(BF16)
    queries = qkv[:, :width].reshape(length, HEADS, HEAD_DIM)
    keys_all = qkv[:, width : 2 * width].reshape(length, HEADS, HEAD_DIM)
    values_all = qkv[:, 2 * width :].reshape(length, HEADS, HEAD_DIM)
    segment_row = segment_ids[0]
    padding_row = padding[0]
    position = jnp.arange(length, dtype=jnp.int32)
    allowed = (
        (segment_row[:, None] == segment_row[None, :])
        & (position[:, None] >= position[None, :])
        & ((padding_row[None, :] == 1) | (position[:, None] == position[None, :]))
    )
    scores = jnp.einsum("qhe,khe->hqk", queries, keys_all, preferred_element_type=F32) * score_scale
    masked = jnp.where(allowed[None], scores, -1000000000.0)
    peak = jnp.max(masked, -1, keepdims=True)
    expanded = jnp.exp(masked - peak)
    attention = expanded / jnp.sum(expanded, -1, keepdims=True)
    attention_low = attention.astype(BF16)
    mixed = jnp.einsum("hqk,khe->qhe", attention_low, values_all, preferred_element_type=F32)
    mixed = mixed.reshape(length, width).astype(BF16)
    mixed_other = lax.ppermute(mixed, "core", SWAP)
    resid = inputs + nn(mixed, out_weight)
    normal2, factor2 = layer_stats(resid)
    second = (normal2 * norm2_gain + norm2_bias).astype(BF16)

    own = nn(compact, exchange(tn(dispatch, second).astype(BF16))).astype(BF16)
    other = lax.ppermute(own, "dp", SWAP)

    hidden = nn(own, up)
    active, slope = gelu_pair(hidden)
    active = active.astype(BF16)
    hidden_grad = (nt(grad_own, down) * slope).astype(BF16)
    input_part = nt(hidden_grad, up).astype(BF16)
    grad_back = exchange(tn(compact, input_part).astype(BF16))
    result = nn(active, down).astype(BF16)
    returned = exchange(tn(compact, result).astype(BF16))
    output = (resid + nn(dispatch, returned)).astype(BF16)

    other_active, other_slope = gelu_pair(nn(other, up))
    other_grad = (nt(grad_other, down) * other_slope).astype(BF16)
    active_all = jnp.concatenate([active, other_active.astype(BF16)], 0)
    grads_all = jnp.concatenate([hidden_grad, other_grad], 0)
    rows_all = jnp.concatenate([own, other], 0)
    result_grads = jnp.concatenate([grad_own, grad_other], 0)
    up_grad = tn(lax.dynamic_slice_in_dim(rows_all, dp * 512, 512, 1), grads_all)
    down_grad = tn(lax.dynamic_slice_in_dim(active_all, dp * 2048, 2048, 1), result_grads)

    second_grad = nn(dispatch, grad_back)
    gain2_grad = jnp.sum(second_grad * normal2, 0)
    bias2_grad = jnp.sum(second_grad, 0)
    resid_grad = cotangent.astype(F32) + norm_back(second_grad, normal2, factor2, norm2_gain)
    branch_grad = resid_grad.astype(BF16)
    keep, came = swap_half(branch_grad, core)
    out_grad = scatter_sum((tn(mixed, keep) + tn(mixed_other, came)).astype(BF16), ("x",))
    mixed_grad = nt(branch_grad, out_weight).astype(BF16).reshape(length, HEADS, HEAD_DIM)

    weight_grad = jnp.einsum("qhe,khe->hqk", mixed_grad, values_all, preferred_element_type=F32)
    score_grad = (
        attention * (weight_grad - jnp.sum(attention * weight_grad, -1, keepdims=True))
    ).astype(BF16)
    query_grad = (
        jnp.einsum("hqk,khe->qhe", score_grad, keys_all, preferred_element_type=F32) * score_scale
    )
    key_grad = (
        jnp.einsum("hqk,qhe->khe", score_grad, queries, preferred_element_type=F32) * score_scale
    )
    value_grad = jnp.einsum("hqk,qhe->khe", attention_low, mixed_grad, preferred_element_type=F32)
    thirds = [g.reshape(length, width).astype(BF16) for g in (query_grad, key_grad, value_grad)]
    parts = []
    for third, axes in zip(thirds, (("x",), ("dp", "yh"), ("z",)), strict=True):
        keep, came = swap_half(third, core)
        parts.append(scatter_sum((tn(normed, keep) + tn(normed_other, came)).astype(BF16), axes))
    qkv_grad_sum = jnp.concatenate(parts, 1)

    normed_grad = nt(jnp.concatenate(thirds, 1), qkv_weight)
    gain1_grad = jnp.sum(normed_grad * normal1, 0)
    bias1_grad = jnp.sum(normed_grad, 0)
    input_grad = resid_grad + norm_back(normed_grad, normal1, factor1, norm1_gain)
    small = jnp.stack([gain1_grad, bias1_grad, gain2_grad, bias2_grad])
    small = small.reshape(4, 128, 8).transpose(1, 0, 2).reshape(128, 32)
    small = jnp.sum(lax.all_to_all(small, SPLIT, 0, 0, tiled=True), 0).reshape(4, 8)
    return (
        output,
        input_grad,
        small[0],
        small[1],
        qkv_grad_sum,
        out_grad,
        small[2],
        small[3],
        up_grad[None],
        down_grad[None],
    )


def solution(mesh):
    fine = Mesh(mesh.devices.reshape(SIZES), SPLIT)
    rows = P(SPLIT, None)
    flat = P(SPLIT)
    experts = P(PEERS, None, None)
    placed = (rows, rows, rows, flat, flat, P(), P(), P(), P(), P(), P(), experts, experts, rows)
    halves = P(PEERS, "dp", None)
    return jax.shard_map(
        shards,
        mesh=fine,
        in_specs=placed,
        out_specs=(rows, rows, flat, flat, rows, rows, flat, flat, halves, halves),
        check_vma=False,
    )
```

```python
import jax
import jax.numpy as jnp
from jax import lax
from jax.experimental import pallas as pl
from jax.experimental.pallas import tpu as pltpu
from jax.sharding import Mesh
from jax.sharding import PartitionSpec as P

HEAD_DIM = 64
SPLIT = ("dp", "x", "z", "yh", "core")
PEERS = ("x", "z", "yh", "core")
SIZES = (2, 4, 4, 2, 2)
SWAP = [(0, 1), (1, 0)]
F32 = jnp.float32
BF16 = jnp.bfloat16
MIB = 1 << 20
SCALE = HEAD_DIM ** (-0.5)
GELU = 0.7978845608028654
CUBE = 0.044715
HBM = pl.BlockSpec(memory_space=pl.ANY)
WORD = pl.BlockSpec(memory_space=pltpu.SMEM)


def mm(a, b, dims):
    return lax.dot_general(a, b, (dims, ((), ())), preferred_element_type=F32)


def nn(a, b):
    return mm(a, b, ((1,), (0,)))


def nt(a, b):
    return mm(a, b, ((1,), (1,)))


def tn(a, b):
    return mm(a, b, ((0,), (0,)))


def layer_stats(values):
    center = values - jnp.mean(values, -1, keepdims=True)
    spread = jnp.mean(center * center, -1, keepdims=True)
    factor = lax.rsqrt(spread + 1e-05)
    return (center * factor, factor)


def norm_back(grad_out, normal, factor, gain):
    grad_hat = grad_out * gain
    return factor * (
        grad_hat
        - jnp.mean(grad_hat, -1, keepdims=True)
        - normal * jnp.mean(grad_hat * normal, -1, keepdims=True)
    )


def gelu_pair(v):
    square = v * v
    half = 0.5 + 0.5 * jnp.tanh(v * (GELU + GELU * CUBE * square))
    slope = half + half * (1.0 - half) * (v * (2 * GELU + 6 * GELU * CUBE * square))
    return v * half, slope


def iota(shape, dim):
    return lax.broadcasted_iota(jnp.int32, shape, dim)


def arr(dtype, *dims):
    return jax.ShapeDtypeStruct(dims, dtype)


def room(dtype, *dims):
    return pltpu.VMEM(dims, dtype)


def sems(n):
    return pltpu.SemaphoreType.DMA((n,))


def whole(*dims):
    return pl.BlockSpec(dims, lambda: (0,) * len(dims))


def call(kernel, name, ins, outs, outs_shape, scratch, flops, mib):
    return pl.pallas_call(
        kernel,
        name=name,
        in_specs=ins,
        out_specs=outs,
        scratch_shapes=scratch,
        out_shape=outs_shape,
        compiler_params=pltpu.CompilerParams(vmem_limit_bytes=62 * MIB),
        cost_estimate=pl.CostEstimate(
            flops=int(flops * 1e9), bytes_accessed=mib * MIB, transcendentals=0
        ),
    )


def begin(src, dst, sem):
    copy = pltpu.make_async_copy(src, dst, sem)
    copy.start()
    return copy


def finish(copies):
    for copy in copies:
        copy.wait()


def message_row(stacked):
    quarter = (stacked * 683) >> 16
    rest = stacked - quarter * 96
    kind = (rest * 1366) >> 16
    rest = rest - kind * 48
    expert_of = (rest * 10923) >> 16
    return expert_of * 48 + quarter * 12 + kind * 6 + (rest - expert_of * 6)


def pack(first, second, out):
    order = (iota((384, 384), 0) == message_row(iota((384, 384), 1))).astype(BF16)
    for g in range(8):
        rows = slice(48 * g, 48 * g + 48)
        parts = []
        for q in range(4):
            cols = slice(256 * q, 256 * q + 256)
            parts += [first[rows, cols], second[rows, cols]]
        out[384 * g : 384 * g + 384] = nn(order, jnp.concatenate(parts, 0)).astype(BF16)


def unpack(message, first, second):
    order = (message_row(iota((384, 384), 0)) == iota((384, 384), 1)).astype(BF16)
    for g in range(8):
        rows = slice(48 * g, 48 * g + 48)
        stack = nn(order, message[384 * g : 384 * g + 384]).astype(BF16)
        for q in range(4):
            cols = slice(256 * q, 256 * q + 256)
            first[rows, cols] = stack[96 * q : 96 * q + 48]
            second[rows, cols] = stack[96 * q + 48 : 96 * q + 96]


def mask_bias(seg_row, pad_row):
    query = iota((256, 256), 0)
    key = iota((256, 256), 1)
    seg_key = jnp.broadcast_to(seg_row.astype(F32), (256, 256))
    allowed = (seg_key.T == seg_key) & (query >= key) & ((pad_row == 1) | (query == key))
    return jnp.where(allowed, 0.0, -1000000000.0)


def slot_rows(expert_ids, slots):
    return (iota((384, 256), 0) == expert_ids * 6 + slots).astype(BF16)


def by_head(block):
    head = iota((256, 256), 1) >> 6
    return jnp.concatenate(
        [jnp.where(head == h, block, jnp.zeros_like(block)) for h in range(4)], 0
    )


def side_by_side(stack):
    return jnp.concatenate([stack[256 * h : 256 * h + 256] for h in range(4)], 1)


def softmax(q_heads, keys, bias):
    masked = (nt(q_heads, keys) * SCALE).reshape(4, 256, 256) + bias[None]
    expanded = jnp.exp(masked - jnp.max(masked, -1, keepdims=True))
    return (expanded * (1.0 / jnp.sum(expanded, -1, keepdims=True))).reshape(1024, 256)


def forward_kernel(
    seg_row, pad_row, expert_ids, slots, gain1, bias1, gain2, bias2, tok_hbm, cot_hbm, qkv_hbm, wo_hbm,
    normed_out, qkv_out, mixed_out, resid_out, send_out,
    tok, cot, w_qkv, wo, normed, qkv, mixed, resid, send, in_sem, out_sem,
):
    def fetch(g):
        if g < 4:
            for n in range(3):
                source = qkv_hbm.at[:, pl.ds(1024 * n + 256 * g, 256)]
                target = w_qkv.at[g, :, pl.ds(256 * n, 256)]
                loads.append(begin(source, target, in_sem.at[1 + 3 * g + n]))
        if g == 4:
            loads.append(begin(wo_hbm, wo, in_sem.at[13]))
        if g == 5:
            loads.append(begin(cot_hbm, cot, in_sem.at[14]))

    loads = [begin(tok_hbm, tok, in_sem.at[0])]
    fetch(0)
    bias = mask_bias(seg_row[...], pad_row[...])
    loads[0].wait()
    fetch(1)
    normal, _ = layer_stats(tok[...].astype(F32))
    normed[...] = (normal * gain1[...] + bias1[...]).astype(BF16)
    stores = [begin(normed, normed_out, out_sem.at[0])]

    def project(g):
        finish(loads[1 + 3 * g : 4 + 3 * g])
        fetch(g + 2)
        qkv[g] = nn(normed[...], w_qkv[g]).astype(BF16)
        stores.append(begin(qkv.at[g], qkv_out.at[g], out_sem.at[1 + g]))

    project(0)
    for g in range(4):
        if g < 3:
            project(g + 1)
        attention = softmax(by_head(qkv[g, :, :256]), qkv[g, :, 256:512], bias)
        attention = side_by_side(attention.astype(BF16))
        mixed[:, 256 * g : 256 * g + 256] = nn(attention, by_head(qkv[g, :, 512:])).astype(BF16)
    stores.append(begin(mixed, mixed_out, out_sem.at[5]))
    loads[13].wait()
    resid[...] = tok[...].astype(F32) + nn(mixed[...], wo[...])
    stores.append(begin(resid, resid_out, out_sem.at[6]))
    normal, _ = layer_stats(resid[...])
    second = (normal * gain2[...] + bias2[...]).astype(BF16)
    dispatch = slot_rows(expert_ids[...], slots[...])
    loads[14].wait()
    pack(nn(dispatch, second).astype(BF16), nn(dispatch, cot[...]).astype(BF16), send)
    stores.append(begin(send, send_out, out_sem.at[7]))
    finish(stores)


def forward(*args):
    line = whole(1, 1024)
    short = whole(1, 256)
    return call(
        forward_kernel, "forward",
        [short] * 4 + [line] * 4 + [HBM] * 4,
        [HBM] * 5,
        [
            arr(BF16, 256, 1024), arr(BF16, 4, 256, 768), arr(BF16, 256, 1024),
            arr(F32, 256, 1024), arr(BF16, 3072, 256),
        ],
        [
            room(BF16, 256, 1024), room(BF16, 256, 1024), room(BF16, 4, 1024, 768),
            room(BF16, 1024, 1024), room(BF16, 256, 1024), room(BF16, 4, 256, 768), room(BF16, 256, 1024),
            room(F32, 256, 1024), room(BF16, 3072, 256), sems(15), sems(8),
        ],
        4, 14,
    )(*args)


def expert_kernel(
    packed_hbm, up_hbm, down_hbm, rows_out, crows_out, active_out, grad_out, send_out,
    packed, rows, crows, up, down, hidden, active, grad, total, send, in_sem, out_sem, one_sem,
):
    def up_copy(i):
        source = up_hbm.at[:, pl.ds(pl.multiple_of(512 * i, 512), 512)]
        return pltpu.make_async_copy(source, up.at[i], in_sem.at[i, 0])

    def down_copy(i):
        source = down_hbm.at[pl.ds(pl.multiple_of(512 * i, 512), 512)]
        return pltpu.make_async_copy(source, down.at[i], in_sem.at[i, 1])

    def active_copy(i):
        return pltpu.make_async_copy(active.at[i], active_out.at[i], out_sem.at[i, 0])

    def grad_copy(i):
        return pltpu.make_async_copy(grad.at[i], grad_out.at[i], out_sem.at[i, 1])

    load_rows = begin(packed_hbm, packed, one_sem.at[0])
    up_copy(0).start()
    load_rows.wait()
    up_copy(1).start()
    down_copy(0).start()
    unpack(packed, rows, crows)
    stores = [begin(rows, rows_out, one_sem.at[1]), begin(crows, crows_out, one_sem.at[2])]
    up_copy(0).wait()
    hidden[0] = nn(rows[...], up[0])

    def layer(i, slot):
        pulled = nt(crows[...], down[i])
        low, slope = gelu_pair(hidden[slot])
        active[i] = low.astype(BF16)
        grad[i] = (pulled * slope).astype(BF16)
        active_copy(i).start()
        grad_copy(i).start()

    def body(i, _):
        up_copy(i + 1).wait()
        down_copy(i).wait()

        @pl.when(i < 6)
        def _():
            up_copy(i + 2).start()

        down_copy(i + 1).start()
        slot = lax.rem(i, 2)
        hidden[1 - slot] = nn(rows[...], up[i + 1])
        layer(i, slot)
        return 0

    lax.fori_loop(0, 7, body, 0)
    down_copy(7).wait()
    layer(7, 1)
    total[0] = nt(grad[0], up[0])
    total[1] = nn(active[0], down[0])

    def outward(i, _):
        total[0] += nt(grad[i], up[i])
        total[1] += nn(active[i], down[i])
        return 0

    lax.fori_loop(1, 8, outward, 0)
    pack(total[0].astype(BF16), total[1].astype(BF16), send)
    stores.append(begin(send, send_out, one_sem.at[3]))

    def drain(i, _):
        active_copy(i).wait()
        grad_copy(i).wait()
        return 0

    lax.fori_loop(0, 8, drain, 0)
    finish(stores)


def expert(packed, up, down):
    rows = arr(BF16, 384, 1024)
    wide = arr(BF16, 8, 384, 512)
    return call(
        expert_kernel, "expert", [HBM] * 3, [HBM] * 5,
        [rows, rows, wide, wide, arr(BF16, 3072, 256)],
        [
            room(BF16, 3072, 256), room(BF16, 384, 1024), room(BF16, 384, 1024),
            room(BF16, 8, 1024, 512), room(BF16, 8, 512, 1024), room(F32, 2, 384, 512),
            room(BF16, 8, 384, 512), room(BF16, 8, 384, 512), room(F32, 2, 384, 1024),
            room(BF16, 3072, 256), pltpu.SemaphoreType.DMA((8, 2)), pltpu.SemaphoreType.DMA((8, 2)), sems(4),
        ],
        14, 30,
    )(packed, up, down)


def weights_kernel(
    dp, own_hbm, grad_own_hbm, packed_hbm, active_hbm, grad_hbm, up_hbm, down_hbm,
    up_out, down_out,
    packed, other, grad_other, halves, result_grads, grads, actives, up, down, up_buf, down_buf,
    one_sem, in_sem, out_sem,
):
    half = pl.ds(pl.multiple_of(dp[0] * 512, 512), 512)
    mine = [pl.ds(pl.multiple_of(dp[0] * 2048 + 256 * i, 256), 256) for i in range(8)]
    rest = [pl.ds(pl.multiple_of((1 - dp[0]) * 2048 + 256 * i, 256), 256) for i in range(8)]
    left = pl.ds(0, 256)
    right = pl.ds(256, 256)
    top = pl.ds(0, 384)
    parts = [pl.ds(i % 2 * 256, 256) for i in range(8)]
    near = [dp[0] * 4 + i // 2 for i in range(8)]
    far = [(1 - dp[0]) * 4 + i // 2 for i in range(8)]
    first = [
        begin(packed_hbm, packed, one_sem.at[0]),
        begin(own_hbm.at[:, half], halves.at[top], one_sem.at[1]),
        begin(grad_own_hbm, result_grads.at[top], one_sem.at[2]),
    ]
    loads = []

    def fetch(i):
        if i < 8:
            loads.append(
                [
                    begin(up_hbm.at[:, mine[i]], up.at[i, :, left], in_sem.at[i, 0]),
                    begin(up_hbm.at[:, rest[i]], up.at[i, :, right], in_sem.at[i, 1]),
                    begin(down_hbm.at[mine[i]], down.at[i, left], in_sem.at[i, 2]),
                    begin(down_hbm.at[rest[i]], down.at[i, right], in_sem.at[i, 3]),
                    begin(grad_hbm.at[near[i], :, parts[i]], grads.at[i, top, left], in_sem.at[i, 4]),
                    begin(grad_hbm.at[far[i], :, parts[i]], grads.at[i, top, right], in_sem.at[i, 5]),
                    begin(active_hbm.at[near[i], :, parts[i]], actives.at[i, top], in_sem.at[i, 6]),
                ]
            )

    fetch(0)
    finish(first)
    fetch(1)
    unpack(packed, other, grad_other)
    halves[384:] = jnp.where(dp[0] == 0, other[:, :512], other[:, 512:])
    result_grads[384:] = grad_other[...]
    stores = []
    for i in range(9):
        if i < 8:
            finish(loads[i])
            fetch(i + 2)
        if i > 2:
            finish(stores[i - 3])
        if i < 8:
            active, slope = gelu_pair(nn(other[...], up[i]))
            actives[i, 384:] = active[:, :256].astype(BF16)
            grads[i, 384:] = (nt(grad_other[...], down[i]) * slope).astype(BF16)
        if i > 0:
            slot = i % 2
            up_buf[slot] = tn(halves[...], grads[i - 1])
            down_buf[slot] = tn(actives[i - 1], result_grads[...])
            stores.append(
                [
                    begin(up_buf.at[slot, :, left], up_out.at[:, mine[i - 1]], out_sem.at[i - 1, 0]),
                    begin(up_buf.at[slot, :, right], up_out.at[:, rest[i - 1]], out_sem.at[i - 1, 1]),
                    begin(down_buf.at[slot], down_out.at[pl.ds(256 * (i - 1), 256)], out_sem.at[i - 1, 2]),
                ]
            )
    finish(stores[6])
    finish(stores[7])


def weights(*args):
    return call(
        weights_kernel, "weights", [WORD] + [HBM] * 7, [HBM, HBM],
        [arr(F32, 512, 4096), arr(F32, 2048, 1024)],
        [
            room(BF16, 3072, 256), room(BF16, 384, 1024), room(BF16, 384, 1024),
            room(BF16, 768, 512), room(BF16, 768, 1024), room(BF16, 8, 768, 512),
            room(BF16, 8, 768, 256), room(BF16, 8, 1024, 512), room(BF16, 8, 512, 1024),
            room(F32, 2, 512, 512), room(F32, 2, 256, 1024), sems(3),
            pltpu.SemaphoreType.DMA((8, 7)), pltpu.SemaphoreType.DMA((8, 3)),
        ],
        13, 46,
    )(*args)


def backward_kernel(
    spot, seg_row, pad_row, expert_ids, slots, gain2, back_hbm, cot_hbm, resid_hbm, wo_hbm, qkv_hbm,
    gain_out, bias_out, out, resid_grad_out, grads_out, keep_x, keep_z, send_x, send_z,
    packed, back, result, cot, resid, wo, qkv, resid_grad, branch, grads, in_sem, out_sem,
):
    firsts = [
        begin(back_hbm, packed, in_sem.at[0]),
        begin(resid_hbm, resid, in_sem.at[1]),
        begin(cot_hbm, cot, in_sem.at[2]),
    ]
    groups = [((1 - spot[0] + i // 2) % 2) * 2 + i % 2 for i in range(4)]
    loads = []

    def fetch(i):
        if i < 4:
            rows = pl.ds(pl.multiple_of(groups[i] * 256, 256), 256)
            loads.append(
                [
                    begin(wo_hbm.at[rows], wo.at[i], in_sem.at[3 + 2 * i]),
                    begin(qkv_hbm.at[groups[i]], qkv.at[i], in_sem.at[4 + 2 * i]),
                ]
            )

    dispatch = slot_rows(expert_ids[...], slots[...])
    bias = mask_bias(seg_row[...], pad_row[...])
    finish(firsts)
    fetch(0)
    fetch(1)
    unpack(packed, back, result)
    second_grad = tn(dispatch, back[...])
    normal, factor = layer_stats(resid[...])
    gain_out[...] = jnp.sum(second_grad * normal, 0, keepdims=True)
    bias_out[...] = jnp.sum(second_grad, 0, keepdims=True)
    grad = cot[...].astype(F32) + norm_back(second_grad, normal, factor, gain2[...])
    resid_grad[...] = grad
    branch[...] = grad.astype(BF16)
    stores = [begin(resid_grad, resid_grad_out, out_sem.at[4, 0])]
    for i in range(4):
        finish(loads[i])
        fetch(i + 2)
        mixed_grad = nt(branch[...], wo[i]).astype(BF16)
        k = qkv[i, :, 256:512]
        q_heads = by_head(qkv[i, :, :256])
        grad_heads = by_head(mixed_grad)
        attention = softmax(q_heads, k, bias)
        pulled = nt(grad_heads, qkv[i, :, 512:])
        inner = jnp.sum(attention * pulled, -1, keepdims=True)
        score_grad = (attention * (pulled - inner)).astype(BF16)
        dq = nn(side_by_side(score_grad), by_head(k))
        dk = tn(score_grad, q_heads)
        dv = tn(attention.astype(BF16), grad_heads)
        grads[i, 0] = (dq * SCALE).astype(BF16)
        grads[i, 1] = (dk * SCALE).astype(BF16)
        grads[i, 2] = dv.astype(BF16)
        grads[i, 3] = branch[:, pl.ds(pl.multiple_of(groups[i] * 256, 256), 256)]
        stores.append(begin(grads.at[i], grads_out.at[i], out_sem.at[i, 4]))
        cols = pl.ds(256 * (i % 2), 256)
        pair_x, pair_z = (send_x, send_z) if i < 2 else (keep_x, keep_z)
        for mine in range(2):
            tensor_x = spot[1] if mine else 1 - spot[1]
            tensor_z = 2 + (spot[2] if mine else 1 - spot[2])
            stores.append(begin(grads.at[i, tensor_x], pair_x[mine].at[:, cols], out_sem.at[i, mine]))
            stores.append(begin(grads.at[i, tensor_z], pair_z[mine].at[:, cols], out_sem.at[i, 2 + mine]))
    out[...] = (resid[...] + tn(dispatch, result[...])).astype(BF16)
    finish(stores)


def backward(*args):
    line = whole(1, 1024)
    short = whole(1, 256)
    pair = [arr(BF16, 256, 512)] * 2
    return call(
        backward_kernel, "backward",
        [WORD, short, short, short, short, line] + [HBM] * 5,
        [line, line, whole(256, 1024), HBM, HBM] + [[HBM, HBM]] * 4,
        [arr(F32, 1, 1024), arr(F32, 1, 1024), arr(BF16, 256, 1024), arr(F32, 256, 1024)]
        + [arr(BF16, 4, 4, 256, 256), pair, pair, pair, pair],
        [
            room(BF16, 3072, 256), room(BF16, 384, 1024), room(BF16, 384, 1024),
            room(BF16, 256, 1024), room(F32, 256, 1024),
            room(BF16, 4, 256, 1024), room(BF16, 4, 256, 768), room(F32, 256, 1024),
            room(BF16, 256, 1024), room(BF16, 4, 4, 256, 256), sems(11),
            pltpu.SemaphoreType.DMA((5, 5)),
        ],
        5, 10,
    )(*args)


def input_kernel(
    spot, gain1, grads_hbm, qkv_hbm, tok_hbm, resid_grad_hbm, gain_out, bias_out, out,
    grads, w_qkv, tok, resid_grad, sem,
):
    loads = []
    for i in range(4):
        col = ((1 - spot[0] + i // 2) % 2) * 512 + i % 2 * 256
        loads.append([])
        for n in range(3):
            here = grads.at[i, :, pl.ds(256 * n, 256)]
            loads[i].append(begin(grads_hbm.at[i, n], here, sem.at[6 * i + n + 3]))
            cols = pl.ds(pl.multiple_of(1024 * n + col, 256), 256)
            part = w_qkv.at[i, :, pl.ds(256 * n, 256)]
            loads[i].append(begin(qkv_hbm.at[:, cols], part, sem.at[6 * i + n]))
    lasts = [begin(tok_hbm, tok, sem.at[24]), begin(resid_grad_hbm, resid_grad, sem.at[25])]
    grad = jnp.zeros((256, 1024), F32)
    for i in range(4):
        finish(loads[i])
        grad = grad + nt(grads[i], w_qkv[i])
    finish(lasts)
    normal, factor = layer_stats(tok[...].astype(F32))
    gain_out[...] = jnp.sum(grad * normal, 0, keepdims=True)
    bias_out[...] = jnp.sum(grad, 0, keepdims=True)
    out[...] = resid_grad[...] + norm_back(grad, normal, factor, gain1[...])


def input_gradient(*args):
    line = whole(1, 1024)
    return call(
        input_kernel, "input_gradient", [WORD, line] + [HBM] * 4,
        [line, line, whole(256, 1024)],
        [arr(F32, 1, 1024), arr(F32, 1, 1024), arr(F32, 256, 1024)],
        [
            room(BF16, 4, 256, 768), room(BF16, 4, 1024, 768), room(BF16, 256, 1024),
            room(F32, 256, 1024), sems(26),
        ],
        1.6, 10,
    )(*args)


def partial_kernel(
    gain1, bias1, gain2, bias2, acts_hbm, grads_hbm, out, acts, grads, sums, small, in_sem, out_sem
):
    loads = [[], []]

    def fetch(j):
        for n in range(4 * j, 4 * j + 4):
            rows = pl.ds(256 * (n % 4), 256)
            loads[j].append(begin(acts_hbm[n], acts.at[j, rows], in_sem.at[n]))
            loads[j].append(begin(grads_hbm[n], grads.at[j, rows], in_sem.at[8 + n]))

    fetch(0)
    lines = [gain1[...], bias1[...], gain2[...], bias2[...], jnp.zeros((124, 1024), F32)]
    small[...] = jnp.concatenate(lines, 0).T.astype(BF16)
    stores = [begin(small, out.at[:, pl.ds(1024, 128)], out_sem.at[2])]
    for j in range(2):
        finish(loads[j])
        if j == 0:
            fetch(1)
        sums[j] = tn(acts[j], grads[j]).astype(BF16)
        stores.append(begin(sums.at[j], out.at[:, pl.ds(512 * j, 512)], out_sem.at[j]))
    finish(stores)


def partial_sums(*args):
    return call(
        partial_kernel, "partial_sums", [whole(1, 1024)] * 4 + [[HBM] * 8] * 2, HBM,
        arr(BF16, 1024, 1152),
        [
            room(BF16, 2, 1024, 1024), room(BF16, 2, 1024, 512), room(BF16, 2, 1024, 512),
            room(BF16, 1024, 128), sems(16), sems(3),
        ],
        2.2, 8,
    )(*args)


def total_kernel(got_hbm, qkv_out, out_out, small_out, got, sem):
    loads = [begin(got_hbm.at[pl.ds(16 * i, 16)], got.at[i], sem.at[i]) for i in range(8)]
    totals = [jnp.zeros((8, 512), F32) for _ in range(8)]
    small = jnp.zeros((8, 128), F32)
    for i in range(8):
        loads[i].wait()
        for n in range(16):
            half = n % 2
            tensor_x = i % 2
            tensor_z = 2 + n // 4 % 2
            rows = got[i, n].astype(F32)
            totals[2 * tensor_x + half] = totals[2 * tensor_x + half] + rows[:, :512]
            totals[2 * tensor_z + half] = totals[2 * tensor_z + half] + rows[:, 512:1024]
            small = small + rows[:, 1024:]
    small_out[...] = small
    for tensor in range(4):
        target, start = (qkv_out, 1024 * tensor) if tensor < 3 else (out_out, 0)
        for half in range(2):
            first = start + 512 * half
            target[:, first : first + 512] = totals[2 * tensor + half]


def total_sums(got):
    return call(
        total_kernel, "total_sums", [HBM], [whole(8, 3072), whole(8, 1024), whole(8, 128)],
        [arr(F32, 8, 3072), arr(F32, 8, 1024), arr(F32, 8, 128)],
        [room(BF16, 8, 16, 8, 1152), sems(8)], 0.01, 2,
    )(got)


def swap_pair(rows, axis):
    return lax.ppermute(rows, axis, [(i, i ^ 1) for i in range(4)])


def swap_pair_across(rows, axis):
    return lax.ppermute(rows, (axis, "core"), [(i, i ^ 3) for i in range(8)])


def exchange(rows):
    got = lax.all_to_all(rows.reshape(64, 48, 256), PEERS, 0, 0, tiled=True)
    return got.reshape(3072, 256)


def swap_core(rows):
    return lax.ppermute(rows, "core", SWAP)


def swap_dp(rows):
    return lax.ppermute(rows, "dp", SWAP)


def tie(*arrays):
    return lax.optimization_barrier(arrays)


def shards(
    tokens,
    segment_ids,
    padding,
    expert_ids,
    slots,
    norm1_gain,
    norm1_bias,
    qkv_weight,
    out_weight,
    norm2_gain,
    norm2_bias,
    up_weight,
    down_weight,
    cotangent,
):
    dp = lax.axis_index("dp").reshape(1)
    core = lax.axis_index("core").reshape(1)
    up = up_weight[0]
    down = down_weight[0]
    gain1 = norm1_gain[None]
    bias1 = norm1_bias[None]
    gain2 = norm2_gain[None]
    bias2 = norm2_bias[None]
    ids = expert_ids[None]
    places = slots[None]

    normed, qkv, mixed, resid, send = forward(
        segment_ids, padding, ids, places,
        gain1, bias1, gain2, bias2, tokens, cotangent, qkv_weight, out_weight,
    )
    odd_x = lax.axis_index("x") % 2
    odd_z = lax.axis_index("z") % 2
    own_z = jnp.where(odd_z == 1, mixed, normed)
    other_z = jnp.where(odd_z == 0, mixed, normed)
    arrived, normed, own_z, other_z = tie(exchange(send), normed, own_z, other_z)
    came = swap_dp(arrived)
    came_x = swap_pair(normed, "x")
    came_z = swap_pair(other_z, "z")
    own, grad_own, active, grads, back = expert(arrived, up, down)
    back, came_x, came_z = tie(back, came_x, came_z)
    acts = [normed, swap_core(normed), came_x, swap_core(came_x)]
    acts += [own_z, swap_core(own_z), came_z, swap_core(came_z)]
    back, came, *acts = tie(exchange(back), came, *acts)
    spot = jnp.stack([core[0], odd_x, odd_z])
    gain2_grad, bias2_grad, output, resid_grad, qkv_grads, keep_x, keep_z, send_x, send_z = backward(
        spot, segment_ids, padding, ids, places, gain2,
        back, cotangent, resid, out_weight, qkv,
    )
    pieces = []
    for axis, keep, send in (("x", keep_x, send_x), ("z", keep_z, send_z)):
        pieces += [keep[1], swap_core(send[1])]
        pieces += [swap_pair(keep[0], axis), swap_pair_across(send[0], axis)]
    gain1_grad, bias1_grad, input_grad = input_gradient(
        spot, gain1, qkv_grads, qkv_weight, tokens, resid_grad
    )
    part = partial_sums(gain1_grad, bias1_grad, gain2_grad, bias2_grad, acts, pieces)
    got = lax.all_to_all(part.reshape(128, 8, 1152), SPLIT, 0, 0, tiled=True)

    came, _ = tie(came, part)
    up_grad, down_grad = weights(dp, own, grad_own, came, active, grads, up, down)
    got, up_grad, down_grad = tie(got, up_grad, down_grad)
    qkv_grad, out_grad, small = total_sums(got)
    return (
        output,
        input_grad,
        small[:, 0],
        small[:, 1],
        qkv_grad,
        out_grad,
        small[:, 2],
        small[:, 3],
        up_grad[None],
        down_grad[None],
    )


def solution(mesh):
    fine = Mesh(mesh.devices.reshape(SIZES), SPLIT)
    rows = P(SPLIT, None)
    flat = P(SPLIT)
    experts = P(PEERS, None, None)
    placed = (rows, rows, rows, flat, flat, P(), P(), P(), P(), P(), P(), experts, experts, rows)
    halves = P(PEERS, "dp", None)
    return jax.shard_map(
        shards,
        mesh=fine,
        in_specs=placed,
        out_specs=(rows, rows, flat, flat, rows, rows, flat, flat, halves, halves),
        check_vma=False,
    )
```

```python
import jax
import jax.numpy as jnp
from jax import lax
from jax.experimental import pallas as pl
from jax.experimental.pallas import tpu as pltpu
from jax.sharding import Mesh
from jax.sharding import PartitionSpec as P

HEAD_DIM = 64
SPLIT = ("dp", "x", "z", "yh", "core")
PEERS = ("x", "z", "yh", "core")
SIZES = (2, 4, 4, 2, 2)
SWAP = [(0, 1), (1, 0)]
F32 = jnp.float32
BF16 = jnp.bfloat16
MIB = 1 << 20
SCALE = HEAD_DIM ** (-0.5)
GELU = 0.7978845608028654
CUBE = 0.044715
HBM = pl.BlockSpec(memory_space=pl.ANY)
WORD = pl.BlockSpec(memory_space=pltpu.SMEM)


def mm(a, b, dims):
    return lax.dot_general(a, b, (dims, ((), ())), preferred_element_type=F32)


def nn(a, b):
    return mm(a, b, ((1,), (0,)))


def nt(a, b):
    return mm(a, b, ((1,), (1,)))


def tn(a, b):
    return mm(a, b, ((0,), (0,)))


def layer_stats(values):
    center = values - jnp.mean(values, -1, keepdims=True)
    spread = jnp.mean(center * center, -1, keepdims=True)
    factor = lax.rsqrt(spread + 1e-05)
    return (center * factor, factor)


def norm_back(grad_out, normal, factor, gain):
    grad_hat = grad_out * gain
    return factor * (
        grad_hat
        - jnp.mean(grad_hat, -1, keepdims=True)
        - normal * jnp.mean(grad_hat * normal, -1, keepdims=True)
    )


def gelu_pair(v):
    square = v * v
    half = 0.5 + 0.5 * jnp.tanh(v * (GELU + GELU * CUBE * square))
    slope = half + half * (1.0 - half) * (v * (2 * GELU + 6 * GELU * CUBE * square))
    return v * half, slope


def iota(shape, dim):
    return lax.broadcasted_iota(jnp.int32, shape, dim)


def arr(dtype, *dims):
    return jax.ShapeDtypeStruct(dims, dtype)


def room(dtype, *dims):
    return pltpu.VMEM(dims, dtype)


def sems(n):
    return pltpu.SemaphoreType.DMA((n,))


def whole(*dims):
    return pl.BlockSpec(dims, lambda: (0,) * len(dims))


def call(kernel, name, ins, outs, outs_shape, scratch, flops, mib, limit=62):
    return pl.pallas_call(
        kernel,
        name=name,
        in_specs=ins,
        out_specs=outs,
        scratch_shapes=scratch,
        out_shape=outs_shape,
        compiler_params=pltpu.CompilerParams(vmem_limit_bytes=limit * MIB),
        cost_estimate=pl.CostEstimate(
            flops=int(flops * 1e9), bytes_accessed=mib * MIB, transcendentals=0
        ),
    )


def begin(src, dst, sem):
    copy = pltpu.make_async_copy(src, dst, sem)
    copy.start()
    return copy


def finish(copies):
    for copy in copies:
        copy.wait()


def message_row(stacked, kinds):
    quarter = (stacked * 683) >> 16
    rest = stacked - quarter * 96
    start = quarter * 6 * kinds
    if kinds == 2:
        kind = (rest * 1366) >> 16
        rest = rest - kind * 48
        start = start + kind * 6
    expert_of = (rest * 10923) >> 16
    return expert_of * 24 * kinds + start + (rest - expert_of * 6)


def pack(kinds, out, done=None):
    count = len(kinds)
    size = 96 // count
    order = (iota((384, 384), 0) == message_row(iota((384, 384), 1), count)).astype(BF16)
    for g in range(4 * count):
        rows = slice(size * g, size * g + size)
        parts = []
        for q in range(4):
            parts += [kind[rows, 256 * q : 256 * q + 256] for kind in kinds]
        out[384 * g : 384 * g + 384] = nn(order, jnp.concatenate(parts, 0)).astype(BF16)
        if done is not None:
            done(g, pl.ds(384 * g, 384))


def unpack(message, kinds):
    count = len(kinds)
    size = 96 // count
    order = (message_row(iota((384, 384), 0), count) == iota((384, 384), 1)).astype(BF16)
    for g in range(4 * count):
        rows = slice(size * g, size * g + size)
        stack = nn(order, message[384 * g : 384 * g + 384]).astype(BF16)
        for q in range(4):
            for n, kind in enumerate(kinds):
                first = 96 * q + size * n
                kind[rows, 256 * q : 256 * q + 256] = stack[first : first + size]


def mask_bias(seg_row, pad_row):
    query = iota((256, 256), 0)
    key = iota((256, 256), 1)
    seg_key = jnp.broadcast_to(seg_row.astype(F32), (256, 256))
    allowed = (seg_key.T == seg_key) & (query >= key) & ((pad_row == 1) | (query == key))
    return jnp.where(allowed, 0.0, -1000000000.0)


def slot_rows(expert_ids, slots):
    return (iota((384, 256), 0) == expert_ids * 6 + slots).astype(BF16)


def by_head(block):
    head = iota((256, 256), 1) >> 6
    return jnp.concatenate(
        [jnp.where(head == h, block, jnp.zeros_like(block)) for h in range(4)], 0
    )


def side_by_side(stack):
    return jnp.concatenate([stack[256 * h : 256 * h + 256] for h in range(4)], 1)


def softmax(q_heads, keys, bias):
    masked = (nt(q_heads, keys) * SCALE).reshape(4, 256, 256) + bias[None]
    expanded = jnp.exp(masked - jnp.max(masked, -1, keepdims=True))
    return (expanded * (1.0 / jnp.sum(expanded, -1, keepdims=True))).reshape(1024, 256)


def forward_kernel(
    ints_hbm, lines_hbm, tok_hbm, cot_hbm, qkv_hbm, wo_hbm,
    normed_out, qkv_out, mixed_out, resid_out, send_out,
    ints, lines, tok, cot, w_qkv, wo, normed, qkv, mixed, resid, send, in_sem, out_sem,
):
    def fetch(g):
        if g < 4:
            for n in range(3):
                source = qkv_hbm.at[:, pl.ds(1024 * n + 256 * g, 256)]
                target = w_qkv.at[g, :, pl.ds(256 * n, 256)]
                loads.append(begin(source, target, in_sem.at[1 + 3 * g + n]))
        if g == 4:
            loads.append(begin(wo_hbm, wo, in_sem.at[13]))
        if g == 5:
            loads.append(begin(cot_hbm, cot, in_sem.at[14]))

    loads = [begin(tok_hbm, tok, in_sem.at[0])]
    smalls = [begin(ints_hbm[n], ints[n], in_sem.at[15 + n]) for n in range(4)]
    smalls += [begin(lines_hbm[n], lines[n], in_sem.at[19 + n]) for n in range(4)]
    seg_row, pad_row, expert_ids, slots = ints
    gain1, bias1, gain2, bias2 = lines
    fetch(0)
    fetch(1)
    finish(smalls)
    bias = mask_bias(seg_row[...], pad_row[...])
    loads[0].wait()
    fetch(2)
    normal, _ = layer_stats(tok[...].astype(F32))
    normed[...] = (normal * gain1[...] + bias1[...]).astype(BF16)
    stores = [begin(normed, normed_out, out_sem.at[0])]

    def project(g):
        finish(loads[1 + 3 * g : 4 + 3 * g])
        fetch(g + 3)
        qkv[g] = nn(normed[...], w_qkv[g]).astype(BF16)
        stores.append(begin(qkv.at[g], qkv_out.at[g], out_sem.at[1 + g]))

    project(0)
    for g in range(4):
        if g < 3:
            project(g + 1)
        attention = softmax(by_head(qkv[g, :, :256]), qkv[g, :, 256:512], bias)
        attention = side_by_side(attention.astype(BF16))
        mixed[:, 256 * g : 256 * g + 256] = nn(attention, by_head(qkv[g, :, 512:])).astype(BF16)
    stores.append(begin(mixed, mixed_out, out_sem.at[5]))
    loads[13].wait()
    resid[...] = tok[...].astype(F32) + nn(mixed[...], wo[...])
    stores.append(begin(resid, resid_out, out_sem.at[6]))
    normal, _ = layer_stats(resid[...])
    second = (normal * gain2[...] + bias2[...]).astype(BF16)
    dispatch = slot_rows(expert_ids[...], slots[...])
    loads[14].wait()

    def store(g, rows):
        stores.append(begin(send.at[rows], send_out.at[rows], out_sem.at[7 + g]))

    pack([nn(dispatch, second).astype(BF16), nn(dispatch, cot[...]).astype(BF16)], send, store)
    finish(stores)


def forward(*args):
    return call(
        forward_kernel, "forward",
        [[HBM] * 4, [HBM] * 4] + [HBM] * 4,
        [HBM] * 5,
        [
            arr(BF16, 256, 1024), arr(BF16, 4, 256, 768), arr(BF16, 256, 1024),
            arr(F32, 256, 1024), arr(BF16, 3072, 256),
        ],
        [
            [room(jnp.int32, 1, 256)] * 4, [room(F32, 1, 1024)] * 4,
            room(BF16, 256, 1024), room(BF16, 256, 1024), room(BF16, 4, 1024, 768),
            room(BF16, 1024, 1024), room(BF16, 256, 1024), room(BF16, 4, 256, 768), room(BF16, 256, 1024),
            room(F32, 256, 1024), room(BF16, 3072, 256), sems(23), sems(15),
        ],
        4, 14,
    )(*args)


def expert_kernel(
    packed_hbm, up_hbm, down_hbm, rows_out, crows_out, active_out, grad_out, send_out,
    packed, rows, crows, up, down, hidden, active, grad, send, in_sem, out_sem, one_sem,
):
    def fetch_up(i):
        if i < 4:
            source = up_hbm.at[:, pl.ds(1024 * i, 1024)]
            load_up.append(begin(source, up.at[i], in_sem.at[i, 0]))

    def fetch_down(i):
        if i < 4:
            source = down_hbm.at[pl.ds(1024 * i, 1024)]
            load_down.append(begin(source, down.at[i], in_sem.at[i, 1]))

    load_up = []
    load_down = []
    load_rows = begin(packed_hbm, packed, one_sem.at[0])
    fetch_up(0)
    load_rows.wait()
    fetch_up(1)
    fetch_down(0)
    unpack(packed, [rows, crows])
    load_up[0].wait()
    hidden[0] = nn(rows[...], up[0])
    stores = [begin(rows, rows_out, one_sem.at[1]), begin(crows, crows_out, one_sem.at[2])]
    for i in range(4):
        load_down[i].wait()
        fetch_down(i + 1)
        if i < 3:
            load_up[i + 1].wait()
            fetch_up(i + 2)
            hidden[(i + 1) % 2] = nn(rows[...], up[i + 1])
        pulled = nt(crows[...], down[i])
        low, slope = gelu_pair(hidden[i % 2])
        active[i] = low.astype(BF16)
        grad[i] = (pulled * slope).astype(BF16)
        for n in range(2):
            cols = pl.ds(512 * n, 512)
            tile = 2 * i + n
            stores.append(begin(active.at[i, :, cols], active_out.at[tile], out_sem.at[tile, 0]))
            stores.append(begin(grad.at[i, :, cols], grad_out.at[tile], out_sem.at[tile, 1]))
    back = jnp.zeros((384, 1024), F32)
    result = jnp.zeros((384, 1024), F32)
    for i in range(4):
        back = back + nt(grad[i], up[i])
    for i in range(4):
        result = result + nn(active[i], down[i])

    def store(g, rows):
        stores.append(begin(send.at[rows], send_out.at[rows], one_sem.at[3 + g]))

    pack([back.astype(BF16), result.astype(BF16)], send, store)
    finish(stores)


def expert(packed, up, down):
    rows = arr(BF16, 384, 1024)
    wide = arr(BF16, 8, 384, 512)
    return call(
        expert_kernel, "expert", [HBM] * 3, [HBM] * 5,
        [rows, rows, wide, wide, arr(BF16, 3072, 256)],
        [
            room(BF16, 3072, 256), room(BF16, 384, 1024), room(BF16, 384, 1024),
            room(BF16, 4, 1024, 1024), room(BF16, 4, 1024, 1024), room(F32, 2, 384, 1024),
            room(BF16, 4, 384, 1024), room(BF16, 4, 384, 1024), room(BF16, 3072, 256),
            pltpu.SemaphoreType.DMA((4, 2)), pltpu.SemaphoreType.DMA((8, 2)), sems(11),
        ],
        11, 30,
    )(packed, up, down)


def weights_kernel(
    dp, own_hbm, grad_own_hbm, packed_hbm, active_hbm, grad_hbm, up_hbm, down_hbm,
    up_out, down_out,
    packed, other, grad_other, halves, result_grads, grads, actives, up, down, up_buf, down_buf,
    one_sem, in_sem, out_sem,
):
    left = pl.ds(0, 256)
    right = pl.ds(256, 256)
    top = pl.ds(0, 384)

    def mine(i):
        return pl.ds(pl.multiple_of(dp[0] * 2048 + 256 * i, 256), 256)

    def rest(i):
        return pl.ds(pl.multiple_of((1 - dp[0]) * 2048 + 256 * i, 256), 256)

    def loads(i):
        part = pl.ds(pl.multiple_of(i % 2 * 256, 256), 256)
        near = dp[0] * 4 + i // 2
        far = (1 - dp[0]) * 4 + i // 2
        pairs = [
            (up_hbm.at[:, mine(i)], up.at[i, :, left]),
            (up_hbm.at[:, rest(i)], up.at[i, :, right]),
            (down_hbm.at[mine(i)], down.at[i, left]),
            (down_hbm.at[rest(i)], down.at[i, right]),
            (grad_hbm.at[near, :, part], grads.at[i, top, left]),
            (grad_hbm.at[far, :, part], grads.at[i, top, right]),
            (active_hbm.at[near, :, part], actives.at[i, top]),
        ]
        return [
            pltpu.make_async_copy(source, target, in_sem.at[i, n])
            for n, (source, target) in enumerate(pairs)
        ]

    def stores(i):
        slot = i % 2
        below = pl.ds(pl.multiple_of(256 * i, 256), 256)
        pairs = [
            (up_buf.at[slot, :, left], up_out.at[:, mine(i)]),
            (up_buf.at[slot, :, right], up_out.at[:, rest(i)]),
            (down_buf.at[slot], down_out.at[below]),
        ]
        return [
            pltpu.make_async_copy(source, target, out_sem.at[i, n])
            for n, (source, target) in enumerate(pairs)
        ]

    def fetch(i):
        for copy in loads(i):
            copy.start()

    def layer(i):
        active, slope = gelu_pair(nn(other[...], up[i]))
        actives[i, 384:] = active[:, :256].astype(BF16)
        grads[i, 384:] = (nt(grad_other[...], down[i]) * slope).astype(BF16)

    def products(i):
        slot = i % 2
        up_buf[slot] = tn(halves[...], grads[i])
        down_buf[slot] = tn(actives[i], result_grads[...])
        for copy in stores(i):
            copy.start()

    half = pl.ds(pl.multiple_of(dp[0] * 512, 512), 512)
    first = [
        begin(packed_hbm, packed, one_sem.at[0]),
        begin(own_hbm.at[:, half], halves.at[top], one_sem.at[1]),
        begin(grad_own_hbm, result_grads.at[top], one_sem.at[2]),
    ]
    fetch(0)
    finish(first)
    fetch(1)
    unpack(packed, [other, grad_other])
    halves[384:] = jnp.where(dp[0] == 0, other[:, :512], other[:, 512:])
    result_grads[384:] = grad_other[...]
    finish(loads(0))
    layer(0)

    def body(i, _):
        finish(loads(i))

        @pl.when(i < 7)
        def _():
            fetch(i + 1)

        @pl.when(i > 2)
        def _():
            finish(stores(i - 3))

        layer(i)
        products(i - 1)
        return 0

    lax.fori_loop(1, 8, body, 0)
    finish(stores(5))
    products(7)
    finish(stores(6))
    finish(stores(7))


def weights(*args):
    return call(
        weights_kernel, "weights", [WORD] + [HBM] * 7, [HBM, HBM],
        [arr(F32, 512, 4096), arr(F32, 2048, 1024)],
        [
            room(BF16, 3072, 256), room(BF16, 384, 1024), room(BF16, 384, 1024),
            room(BF16, 768, 512), room(BF16, 768, 1024), room(BF16, 8, 768, 512),
            room(BF16, 8, 768, 256), room(BF16, 8, 1024, 512), room(BF16, 8, 512, 1024),
            room(F32, 2, 512, 512), room(F32, 2, 256, 1024), sems(3),
            pltpu.SemaphoreType.DMA((8, 7)), pltpu.SemaphoreType.DMA((8, 3)),
        ],
        13, 46,
    )(*args)


def backward_kernel(
    spot, ints_hbm, gain2_hbm, back_hbm, cot_hbm, resid_hbm, wo_hbm, qkv_hbm,
    gain_out, bias_out, out_hbm, resid_grad_out, grads_out, keep_x, keep_z, send_x, send_z,
    ints, gain2, sums, out, packed, back, result, cot, resid, wo, qkv, resid_grad, branch, grads, in_sem, out_sem,
):
    load_packed = begin(back_hbm, packed, in_sem.at[0])
    smalls = [begin(ints_hbm[n], ints[n], in_sem.at[11 + n]) for n in range(4)]
    smalls.append(begin(gain2_hbm, gain2, in_sem.at[15]))
    seg_row, pad_row, expert_ids, slots = ints
    firsts = [begin(resid_hbm, resid, in_sem.at[1]), begin(cot_hbm, cot, in_sem.at[2])]
    groups = [((1 - spot[0] + i // 2) % 2) * 2 + i % 2 for i in range(4)]
    loads = []

    def fetch(i):
        if i < 4:
            rows = pl.ds(pl.multiple_of(groups[i] * 256, 256), 256)
            loads.append(
                [
                    begin(wo_hbm.at[rows], wo.at[i], in_sem.at[3 + 2 * i]),
                    begin(qkv_hbm.at[groups[i]], qkv.at[i], in_sem.at[4 + 2 * i]),
                ]
            )

    finish(smalls)
    dispatch = slot_rows(expert_ids[...], slots[...])
    bias = mask_bias(seg_row[...], pad_row[...])
    load_packed.wait()
    fetch(0)
    unpack(packed, [back, result])
    second_grad = tn(dispatch, back[...])
    finish(firsts)
    fetch(1)
    normal, factor = layer_stats(resid[...])
    sums[0][...] = jnp.sum(second_grad * normal, 0, keepdims=True)
    sums[1][...] = jnp.sum(second_grad, 0, keepdims=True)
    grad = cot[...].astype(F32) + norm_back(second_grad, normal, factor, gain2[...])
    resid_grad[...] = grad
    branch[...] = grad.astype(BF16)
    out[...] = (resid[...] + tn(dispatch, result[...])).astype(BF16)
    stores = [
        begin(resid_grad, resid_grad_out, out_sem.at[4, 0]),
        begin(sums[0], gain_out, out_sem.at[4, 1]),
        begin(sums[1], bias_out, out_sem.at[4, 2]),
        begin(out, out_hbm, out_sem.at[4, 3]),
    ]
    for i in range(4):
        finish(loads[i])
        fetch(i + 2)
        mixed_grad = nt(branch[...], wo[i]).astype(BF16)
        k = qkv[i, :, 256:512]
        q_heads = by_head(qkv[i, :, :256])
        grad_heads = by_head(mixed_grad)
        attention = softmax(q_heads, k, bias)
        pulled = nt(grad_heads, qkv[i, :, 512:])
        inner = jnp.sum(attention * pulled, -1, keepdims=True)
        score_grad = (attention * (pulled - inner)).astype(BF16)
        dq = nn(side_by_side(score_grad), by_head(k))
        dk = tn(score_grad, q_heads)
        dv = tn(attention.astype(BF16), grad_heads)
        grads[i, 0] = (dq * SCALE).astype(BF16)
        grads[i, 1] = (dk * SCALE).astype(BF16)
        grads[i, 2] = dv.astype(BF16)
        grads[i, 3] = branch[:, pl.ds(pl.multiple_of(groups[i] * 256, 256), 256)]
        stores.append(begin(grads.at[i, pl.ds(0, 3)], grads_out.at[i], out_sem.at[i, 4]))
        cols = pl.ds(256 * (i % 2), 256)
        pair_x, pair_z = (send_x, send_z) if i < 2 else (keep_x, keep_z)
        for mine in range(2):
            tensor_x = spot[1] if mine else 1 - spot[1]
            tensor_z = 2 + (spot[2] if mine else 1 - spot[2])
            stores.append(begin(grads.at[i, tensor_x], pair_x[mine].at[:, cols], out_sem.at[i, mine]))
            stores.append(begin(grads.at[i, tensor_z], pair_z[mine].at[:, cols], out_sem.at[i, 2 + mine]))
    finish(stores)


def backward(*args):
    pair = [arr(BF16, 256, 512)] * 2
    return call(
        backward_kernel, "backward",
        [WORD, [HBM] * 4] + [HBM] * 6,
        [HBM] * 5 + [[HBM, HBM]] * 4,
        [arr(F32, 1, 1024), arr(F32, 1, 1024), arr(BF16, 256, 1024), arr(F32, 256, 1024)]
        + [arr(BF16, 4, 3, 256, 256), pair, pair, pair, pair],
        [
            [room(jnp.int32, 1, 256)] * 4, room(F32, 1, 1024), [room(F32, 1, 1024)] * 2,
            room(BF16, 256, 1024), room(BF16, 3072, 256), room(BF16, 384, 1024), room(BF16, 384, 1024),
            room(BF16, 256, 1024), room(F32, 256, 1024),
            room(BF16, 4, 256, 1024), room(BF16, 4, 256, 768), room(F32, 256, 1024),
            room(BF16, 256, 1024), room(BF16, 4, 4, 256, 256), sems(16),
            pltpu.SemaphoreType.DMA((5, 5)),
        ],
        5, 10, 62,
    )(*args)


def input_kernel(
    spot, gain1_hbm, grads_hbm, qkv_hbm, tok_hbm, resid_grad_hbm, gain_out, bias_out, out_hbm,
    gain1, sums, out, grads, w_qkv, tok, resid_grad, sem,
):
    loads = []
    for i in range(4):
        col = ((1 - spot[0] + i // 2) % 2) * 512 + i % 2 * 256
        loads.append([])
        for n in range(3):
            here = grads.at[i, :, pl.ds(256 * n, 256)]
            loads[i].append(begin(grads_hbm.at[i, n], here, sem.at[6 * i + n + 3]))
            cols = pl.ds(pl.multiple_of(1024 * n + col, 256), 256)
            part = w_qkv.at[i, :, pl.ds(256 * n, 256)]
            loads[i].append(begin(qkv_hbm.at[:, cols], part, sem.at[6 * i + n]))
    lasts = [begin(gain1_hbm, gain1, sem.at[26]), begin(tok_hbm, tok, sem.at[24]), begin(resid_grad_hbm, resid_grad, sem.at[25])]
    grad = jnp.zeros((256, 1024), F32)
    for i in range(4):
        finish(loads[i])
        grad = grad + nt(grads[i], w_qkv[i])
    finish(lasts)
    normal, factor = layer_stats(tok[...].astype(F32))
    sums[0][...] = jnp.sum(grad * normal, 0, keepdims=True)
    sums[1][...] = jnp.sum(grad, 0, keepdims=True)
    out[...] = resid_grad[...] + norm_back(grad, normal, factor, gain1[...])
    stores = [
        begin(out, out_hbm, sem.at[27]),
        begin(sums[0], gain_out, sem.at[28]),
        begin(sums[1], bias_out, sem.at[29]),
    ]
    finish(stores)


def input_gradient(*args):
    return call(
        input_kernel, "input_gradient", [WORD] + [HBM] * 5, [HBM] * 3,
        [arr(F32, 1, 1024), arr(F32, 1, 1024), arr(F32, 256, 1024)],
        [
            room(F32, 1, 1024), [room(F32, 1, 1024)] * 2, room(F32, 256, 1024),
            room(BF16, 4, 256, 768), room(BF16, 4, 1024, 768), room(BF16, 256, 1024),
            room(F32, 256, 1024), sems(30),
        ],
        1.6, 10, 62,
    )(*args)


def partial_kernel(
    lines_hbm, acts_hbm, grads_hbm, out, lines, acts, grads, sums, small, in_sem, out_sem
):
    loads = []

    def fetch(n):
        if n < 8:
            rows = pl.ds(256 * (n % 4), 256)
            load = begin(acts_hbm[n], acts.at[n // 4, rows], in_sem.at[n])
            loads.append([load, begin(grads_hbm[n], grads.at[n // 4, rows], in_sem.at[8 + n])])

    for n in range(4):
        fetch(n)
    finish([begin(lines_hbm[n], lines[n], in_sem.at[16 + n]) for n in range(4)])
    rows = [line[...] for line in lines] + [jnp.zeros((124, 1024), F32)]
    small[...] = jnp.concatenate(rows, 0).T.astype(BF16)
    stores = [begin(small, out.at[:, pl.ds(1024, 128)], out_sem.at[2])]
    for j in range(2):
        total = jnp.zeros((1024, 512), F32)
        for half in range(2):
            first = 4 * j + 2 * half
            for n in (first, first + 1):
                finish(loads[n])
            fetch(first + 4)
            fetch(first + 5)
            rows = slice(512 * half, 512 * half + 512)
            total = total + tn(acts[j, rows], grads[j, rows])
        sums[j] = total.astype(BF16)
        stores.append(begin(sums.at[j], out.at[:, pl.ds(512 * j, 512)], out_sem.at[j]))
    finish(stores)


def partial_sums(*args):
    return call(
        partial_kernel, "partial_sums", [[HBM] * 4, [HBM] * 8, [HBM] * 8], HBM,
        arr(BF16, 1024, 1152),
        [
            [room(F32, 1, 1024)] * 4, room(BF16, 2, 1024, 1024), room(BF16, 2, 1024, 512), room(BF16, 2, 1024, 512),
            room(BF16, 1024, 128), sems(20), sems(3),
        ],
        2.2, 8, 62,
    )(*args)


def total_kernel(got_hbm, qkv_out, out_out, gain1, bias1, gain2, bias2, got, sem):
    loads = [begin(got_hbm.at[pl.ds(16 * i, 16)], got.at[i], sem.at[i]) for i in range(8)]
    totals = [jnp.zeros((8, 512), F32) for _ in range(8)]
    small = jnp.zeros((8, 128), F32)
    for i in range(8):
        loads[i].wait()
        for n in range(16):
            half = n % 2
            tensor_x = i % 2
            tensor_z = 2 + n // 4 % 2
            rows = got[i, n].astype(F32)
            totals[2 * tensor_x + half] = totals[2 * tensor_x + half] + rows[:, :512]
            totals[2 * tensor_z + half] = totals[2 * tensor_z + half] + rows[:, 512:1024]
            small = small + rows[:, 1024:]
    small = small.T
    for n, line in enumerate((gain1, bias1, gain2, bias2)):
        line[...] = small[n : n + 1, :]
    for tensor in range(4):
        target, start = (qkv_out, 1024 * tensor) if tensor < 3 else (out_out, 0)
        for half in range(2):
            first = start + 512 * half
            target[:, first : first + 512] = totals[2 * tensor + half]


def total_sums(got):
    return call(
        total_kernel, "total_sums", [HBM], [whole(8, 3072), whole(8, 1024)] + [whole(1, 8)] * 4,
        [arr(F32, 8, 3072), arr(F32, 8, 1024)] + [arr(F32, 1, 8)] * 4,
        [room(BF16, 8, 16, 8, 1152), sems(8)], 0.01, 2, 62,
    )(got)


def swap_pair(rows, axis):
    return lax.ppermute(rows, axis, [(i, i ^ 1) for i in range(4)])


def swap_pair_across(rows, axis):
    return lax.ppermute(rows, (axis, "core"), [(i, i ^ 3) for i in range(8)])


def exchange(rows):
    got = lax.all_to_all(rows.reshape(64, -1, 256), PEERS, 0, 0, tiled=True)
    return got.reshape(-1, 256)


def swap_core(rows):
    return lax.ppermute(rows, "core", SWAP)


def swap_dp(rows):
    return lax.ppermute(rows, "dp", SWAP)


def tie(*arrays):
    return lax.optimization_barrier(arrays)


def shards(
    tokens,
    segment_ids,
    padding,
    expert_ids,
    slots,
    norm1_gain,
    norm1_bias,
    qkv_weight,
    out_weight,
    norm2_gain,
    norm2_bias,
    up_weight,
    down_weight,
    cotangent,
):
    dp = lax.axis_index("dp").reshape(1)
    core = lax.axis_index("core").reshape(1)
    up = up_weight[0]
    down = down_weight[0]
    gain1 = norm1_gain[None]
    bias1 = norm1_bias[None]
    gain2 = norm2_gain[None]
    bias2 = norm2_bias[None]
    ids = expert_ids[None]
    places = slots[None]

    ints = [segment_ids, padding, ids, places]
    lines = [gain1, bias1, gain2, bias2]
    normed, qkv, mixed, resid, send = forward(
        ints, lines, tokens, cotangent, qkv_weight, out_weight
    )
    odd_x = lax.axis_index("x") % 2
    odd_z = lax.axis_index("z") % 2
    own_z = jnp.where(odd_z == 1, mixed, normed)
    other_z = jnp.where(odd_z == 0, mixed, normed)
    arrived, normed, own_z, other_z = tie(exchange(send), normed, own_z, other_z)
    came = swap_dp(arrived)
    came_x = swap_pair(normed, "x")
    came_z = swap_pair(other_z, "z")
    own, grad_own, active, grads, back = expert(arrived, up, down)
    back, came_x, came_z = tie(back, came_x, came_z)
    acts = [normed, swap_core(normed), came_x, swap_core(came_x)]
    acts += [own_z, swap_core(own_z), came_z, swap_core(came_z)]
    spot = jnp.stack([core[0], odd_x, odd_z])
    back, came, *acts = tie(exchange(back), came, *acts)
    gain2_grad, bias2_grad, output, resid_grad, qkv_grads, keep_x, keep_z, send_x, send_z = backward(
        spot, ints, gain2, back, cotangent, resid, out_weight, qkv,
    )
    pieces = []
    for axis, keep, send in (("x", keep_x, send_x), ("z", keep_z, send_z)):
        pieces += [keep[1], swap_core(send[1])]
        pieces += [swap_pair(keep[0], axis), swap_pair_across(send[0], axis)]
    gain1_grad, bias1_grad, input_grad = input_gradient(
        spot, gain1, qkv_grads, qkv_weight, tokens, resid_grad
    )
    part = partial_sums([gain1_grad, bias1_grad, gain2_grad, bias2_grad], acts, pieces)
    got = lax.all_to_all(part.reshape(128, 8, 1152), SPLIT, 0, 0, tiled=True)

    came, _ = tie(came, part)
    up_grad, down_grad = weights(dp, own, grad_own, came, active, grads, up, down)
    got, up_grad, down_grad = tie(got, up_grad, down_grad)
    qkv_grad, out_grad, *small = total_sums(got)
    return (
        output,
        input_grad,
        small[0][0],
        small[1][0],
        qkv_grad,
        out_grad,
        small[2][0],
        small[3][0],
        up_grad[None],
        down_grad[None],
    )


def solution(mesh):
    fine = Mesh(mesh.devices.reshape(SIZES), SPLIT)
    rows = P(SPLIT, None)
    flat = P(SPLIT)
    experts = P(PEERS, None, None)
    placed = (rows, rows, rows, flat, flat, P(), P(), P(), P(), P(), P(), experts, experts, rows)
    halves = P(PEERS, "dp", None)
    return jax.shard_map(
        shards,
        mesh=fine,
        in_specs=placed,
        out_specs=(rows, rows, flat, flat, rows, rows, flat, flat, halves, halves),
        check_vma=False,
    )
```

```python
import jax
import jax.numpy as jnp
from jax import lax
from jax.experimental import pallas as pl
from jax.experimental.pallas import tpu as pltpu
from jax.sharding import Mesh
from jax.sharding import PartitionSpec as P

HEAD_DIM = 64
SPLIT = ("dp", "x", "z", "yh", "core")
PEERS = ("x", "z", "yh", "core")
SIZES = (2, 4, 4, 2, 2)
SWAP = [(0, 1), (1, 0)]
F32 = jnp.float32
BF16 = jnp.bfloat16
MIB = 1 << 20
SCALE = HEAD_DIM ** (-0.5)
GELU = 0.7978845608028654
CUBE = 0.044715
HBM = pl.BlockSpec(memory_space=pl.ANY)
WORD = pl.BlockSpec(memory_space=pltpu.SMEM)


def mm(a, b, dims):
    return lax.dot_general(a, b, (dims, ((), ())), preferred_element_type=F32)


def nn(a, b):
    return mm(a, b, ((1,), (0,)))


def nt(a, b):
    return mm(a, b, ((1,), (1,)))


def tn(a, b):
    return mm(a, b, ((0,), (0,)))


def layer_stats(values):
    center = values - jnp.mean(values, -1, keepdims=True)
    spread = jnp.mean(center * center, -1, keepdims=True)
    factor = lax.rsqrt(spread + 1e-05)
    return (center * factor, factor)


def norm_back(grad_out, normal, factor, gain):
    grad_hat = grad_out * gain
    return factor * (
        grad_hat
        - jnp.mean(grad_hat, -1, keepdims=True)
        - normal * jnp.mean(grad_hat * normal, -1, keepdims=True)
    )


def gelu_pair(v):
    square = v * v
    half = 0.5 + 0.5 * jnp.tanh(v * (GELU + GELU * CUBE * square))
    slope = half + half * (1.0 - half) * (v * (2 * GELU + 6 * GELU * CUBE * square))
    return v * half, slope


def iota(shape, dim):
    return lax.broadcasted_iota(jnp.int32, shape, dim)


def arr(dtype, *dims):
    return jax.ShapeDtypeStruct(dims, dtype)


def room(dtype, *dims):
    return pltpu.VMEM(dims, dtype)


def sems(n):
    return pltpu.SemaphoreType.DMA((n,))


def whole(*dims):
    return pl.BlockSpec(dims, lambda: (0,) * len(dims))


def call(kernel, name, ins, outs, outs_shape, scratch, flops, mib, limit=127):
    return pl.pallas_call(
        kernel,
        name=name,
        in_specs=ins,
        out_specs=outs,
        scratch_shapes=scratch,
        out_shape=outs_shape,
        compiler_params=pltpu.CompilerParams(vmem_limit_bytes=limit * MIB // 2),
        cost_estimate=pl.CostEstimate(
            flops=int(flops * 1e9), bytes_accessed=mib * MIB, transcendentals=0
        ),
    )


def begin(src, dst, sem):
    copy = pltpu.make_async_copy(src, dst, sem)
    copy.start()
    return copy


def finish(copies):
    for copy in copies:
        copy.wait()


def message_row(stacked, kinds):
    quarter = (stacked * 683) >> 16
    rest = stacked - quarter * 96
    start = quarter * 6 * kinds
    if kinds == 2:
        kind = (rest * 1366) >> 16
        rest = rest - kind * 48
        start = start + kind * 6
    expert_of = (rest * 10923) >> 16
    return expert_of * 24 * kinds + start + (rest - expert_of * 6)


def pack(kinds, out, done=None):
    count = len(kinds)
    size = 96 // count
    order = (iota((384, 384), 0) == message_row(iota((384, 384), 1), count)).astype(BF16)
    for g in range(4 * count):
        rows = slice(size * g, size * g + size)
        parts = []
        for q in range(4):
            parts += [kind[rows, 256 * q : 256 * q + 256] for kind in kinds]
        out[384 * g : 384 * g + 384] = nn(order, jnp.concatenate(parts, 0)).astype(BF16)
        if done is not None:
            done(g, pl.ds(384 * g, 384))


def unpack(message, kinds):
    count = len(kinds)
    size = 96 // count
    order = (message_row(iota((384, 384), 0), count) == iota((384, 384), 1)).astype(BF16)
    for g in range(4 * count):
        rows = slice(size * g, size * g + size)
        stack = nn(order, message[384 * g : 384 * g + 384]).astype(BF16)
        for q in range(4):
            for n, kind in enumerate(kinds):
                first = 96 * q + size * n
                kind[rows, 256 * q : 256 * q + 256] = stack[first : first + size]


def unpack_one(message, rows, kind):
    row = iota((192, 384), 0)
    row = row + ((row * 1366) >> 16) * 48 + 48 * kind
    order = (message_row(row, 2) == iota((192, 384), 1)).astype(BF16)
    for g in range(8):
        stack = nn(order, message[384 * g : 384 * g + 384]).astype(BF16)
        for q in range(4):
            part = stack[48 * q : 48 * q + 48]
            rows[48 * g : 48 * g + 48, 256 * q : 256 * q + 256] = part


def mask_bias(seg_row, pad_row):
    query = iota((256, 256), 0)
    key = iota((256, 256), 1)
    seg_key = jnp.broadcast_to(seg_row.astype(F32), (256, 256))
    allowed = (seg_key.T == seg_key) & (query >= key) & ((pad_row == 1) | (query == key))
    return jnp.where(allowed, 0.0, -1000000000.0)


def slot_rows(expert_ids, slots):
    return (iota((384, 256), 0) == expert_ids * 6 + slots).astype(BF16)


def by_head(block):
    head = iota((256, 256), 1) >> 6
    return jnp.concatenate(
        [jnp.where(head == h, block, jnp.zeros_like(block)) for h in range(4)], 0
    )


def side_by_side(stack):
    return jnp.concatenate([stack[256 * h : 256 * h + 256] for h in range(4)], 1)


def softmax(q_heads, keys, bias):
    masked = (nt(q_heads, keys) * SCALE).reshape(4, 256, 256) + bias[None]
    expanded = jnp.exp(masked - jnp.max(masked, -1, keepdims=True))
    return (expanded * (1.0 / jnp.sum(expanded, -1, keepdims=True))).reshape(1024, 256)


def forward_kernel(
    ints_hbm, lines_hbm, tok_hbm, cot_hbm, qkv_hbm, wo_hbm,
    normed_out, qkv_out, mixed_out, resid_out, send_out,
    ints, lines, tok, cot, w_qkv, wo, normed, qkv, mixed, resid, send, in_sem, out_sem,
):
    def fetch(g):
        if g < 4:
            for n in range(3):
                source = qkv_hbm.at[:, pl.ds(1024 * n + 256 * g, 256)]
                target = w_qkv.at[g, :, pl.ds(256 * n, 256)]
                loads.append(begin(source, target, in_sem.at[1 + 3 * g + n]))
        if g == 4:
            loads.append(begin(wo_hbm, wo, in_sem.at[13]))
        if g == 5:
            loads.append(begin(cot_hbm, cot, in_sem.at[14]))

    loads = [begin(tok_hbm, tok, in_sem.at[0])]
    smalls = [begin(ints_hbm[n], ints[n], in_sem.at[15 + n]) for n in range(4)]
    smalls += [begin(lines_hbm[n], lines[n], in_sem.at[19 + n]) for n in range(4)]
    seg_row, pad_row, expert_ids, slots = ints
    gain1, bias1, gain2, bias2 = lines
    fetch(0)
    fetch(1)
    finish(smalls)
    bias = mask_bias(seg_row[...], pad_row[...])
    loads[0].wait()
    fetch(2)
    normal, _ = layer_stats(tok[...].astype(F32))
    normed[...] = (normal * gain1[...] + bias1[...]).astype(BF16)
    stores = [begin(normed, normed_out, out_sem.at[0])]

    def project(g):
        finish(loads[1 + 3 * g : 4 + 3 * g])
        fetch(g + 3)
        qkv[g] = nn(normed[...], w_qkv[g]).astype(BF16)
        stores.append(begin(qkv.at[g], qkv_out.at[g], out_sem.at[1 + g]))

    project(0)
    for g in range(4):
        if g < 3:
            project(g + 1)
        attention = softmax(by_head(qkv[g, :, :256]), qkv[g, :, 256:512], bias)
        attention = side_by_side(attention.astype(BF16))
        mixed[:, 256 * g : 256 * g + 256] = nn(attention, by_head(qkv[g, :, 512:])).astype(BF16)
    stores.append(begin(mixed, mixed_out, out_sem.at[5]))
    loads[13].wait()
    resid[...] = tok[...].astype(F32) + nn(mixed[...], wo[...])
    stores.append(begin(resid, resid_out, out_sem.at[6]))
    normal, _ = layer_stats(resid[...])
    second = (normal * gain2[...] + bias2[...]).astype(BF16)
    dispatch = slot_rows(expert_ids[...], slots[...])
    loads[14].wait()

    def store(g, rows):
        stores.append(begin(send.at[rows], send_out.at[rows], out_sem.at[7 + g]))

    pack([nn(dispatch, second).astype(BF16), nn(dispatch, cot[...]).astype(BF16)], send, store)
    finish(stores)


def forward(*args):
    return call(
        forward_kernel, "forward",
        [[HBM] * 4, [HBM] * 4] + [HBM] * 4,
        [HBM] * 5,
        [
            arr(BF16, 256, 1024), arr(BF16, 4, 256, 768), arr(BF16, 256, 1024),
            arr(F32, 256, 1024), arr(BF16, 3072, 256),
        ],
        [
            [room(jnp.int32, 1, 256)] * 4, [room(F32, 1, 1024)] * 4,
            room(BF16, 256, 1024), room(BF16, 256, 1024), room(BF16, 4, 1024, 768),
            room(BF16, 1024, 1024), room(BF16, 256, 1024), room(BF16, 4, 256, 768), room(BF16, 256, 1024),
            room(F32, 256, 1024), room(BF16, 3072, 256), sems(23), sems(15),
        ],
        4, 14,
    )(*args)


def expert_kernel(
    packed_hbm, up_hbm, down_hbm, rows_out, crows_out, active_out, grad_out, send_out,
    packed, rows, crows, up, down, hidden, active, grad, send, in_sem, out_sem, one_sem,
):
    def fetch_up(i):
        if i < 4:
            source = up_hbm.at[:, pl.ds(1024 * i, 1024)]
            load_up.append(begin(source, up.at[i], in_sem.at[i, 0]))

    def fetch_down(i):
        if i < 4:
            source = down_hbm.at[pl.ds(1024 * i, 1024)]
            load_down.append(begin(source, down.at[i], in_sem.at[i, 1]))

    load_up = []
    load_down = []
    load_rows = begin(packed_hbm, packed, one_sem.at[0])
    fetch_up(0)
    load_rows.wait()
    fetch_up(1)
    fetch_down(0)
    unpack(packed, [rows, crows])
    load_up[0].wait()
    hidden[0] = nn(rows[...], up[0])
    stores = [begin(rows, rows_out, one_sem.at[1]), begin(crows, crows_out, one_sem.at[2])]
    for i in range(4):
        load_down[i].wait()
        fetch_down(i + 1)
        if i < 3:
            load_up[i + 1].wait()
            fetch_up(i + 2)
            hidden[(i + 1) % 2] = nn(rows[...], up[i + 1])
        pulled = nt(crows[...], down[i])
        low, slope = gelu_pair(hidden[i % 2])
        active[i] = low.astype(BF16)
        grad[i] = (pulled * slope).astype(BF16)
        for n in range(2):
            cols = pl.ds(512 * n, 512)
            tile = 2 * i + n
            stores.append(begin(active.at[i, :, cols], active_out.at[tile], out_sem.at[tile, 0]))
            stores.append(begin(grad.at[i, :, cols], grad_out.at[tile], out_sem.at[tile, 1]))
    back = jnp.zeros((384, 1024), F32)
    result = jnp.zeros((384, 1024), F32)
    for i in range(4):
        back = back + nt(grad[i], up[i])
    for i in range(4):
        result = result + nn(active[i], down[i])

    def store(g, rows):
        stores.append(begin(send.at[rows], send_out.at[rows], one_sem.at[3 + g]))

    pack([back.astype(BF16), result.astype(BF16)], send, store)
    finish(stores)


def expert(packed, up, down):
    rows = arr(BF16, 384, 1024)
    wide = arr(BF16, 8, 384, 512)
    return call(
        expert_kernel, "expert", [HBM] * 3, [HBM] * 5,
        [rows, rows, wide, wide, arr(BF16, 3072, 256)],
        [
            room(BF16, 3072, 256), room(BF16, 384, 1024), room(BF16, 384, 1024),
            room(BF16, 4, 1024, 1024), room(BF16, 4, 1024, 1024), room(F32, 2, 384, 1024),
            room(BF16, 4, 384, 1024), room(BF16, 4, 384, 1024), room(BF16, 3072, 256),
            pltpu.SemaphoreType.DMA((4, 2)), pltpu.SemaphoreType.DMA((8, 2)), sems(11),
        ],
        11, 30,
    )(packed, up, down)


def weights_kernel(
    dp, own_hbm, grad_own_hbm, packed_hbm, active_hbm, grad_hbm, up_hbm, down_hbm,
    up_out, down_out,
    packed, other, grad_other, halves, result_grads, grads, actives, up, down, up_buf, down_buf,
    one_sem, in_sem, out_sem,
):
    left = pl.ds(0, 256)
    right = pl.ds(256, 256)
    top = pl.ds(0, 384)

    def mine(i):
        return pl.ds(pl.multiple_of(dp[0] * 2048 + 256 * i, 256), 256)

    def rest(i):
        return pl.ds(pl.multiple_of((1 - dp[0]) * 2048 + 256 * i, 256), 256)

    def loads(i):
        part = pl.ds(pl.multiple_of(i % 2 * 256, 256), 256)
        near = dp[0] * 4 + i // 2
        far = (1 - dp[0]) * 4 + i // 2
        pairs = [
            (up_hbm.at[:, mine(i)], up.at[i, :, left]),
            (up_hbm.at[:, rest(i)], up.at[i, :, right]),
            (down_hbm.at[mine(i)], down.at[i, left]),
            (down_hbm.at[rest(i)], down.at[i, right]),
            (grad_hbm.at[near, :, part], grads.at[i, top, left]),
            (grad_hbm.at[far, :, part], grads.at[i, top, right]),
            (active_hbm.at[near, :, part], actives.at[i, top]),
        ]
        return [
            pltpu.make_async_copy(source, target, in_sem.at[i, n])
            for n, (source, target) in enumerate(pairs)
        ]

    def stores(i):
        slot = i % 2
        below = pl.ds(pl.multiple_of(256 * i, 256), 256)
        pairs = [
            (up_buf.at[slot, :, left], up_out.at[:, mine(i)]),
            (up_buf.at[slot, :, right], up_out.at[:, rest(i)]),
            (down_buf.at[slot], down_out.at[below]),
        ]
        return [
            pltpu.make_async_copy(source, target, out_sem.at[i, n])
            for n, (source, target) in enumerate(pairs)
        ]

    def fetch(i):
        for copy in loads(i):
            copy.start()

    def layer(i):
        active, slope = gelu_pair(nn(other[...], up[i]))
        actives[i, 384:] = active[:, :256].astype(BF16)
        grads[i, 384:] = (nt(grad_other[...], down[i]) * slope).astype(BF16)

    def products(i):
        slot = i % 2
        up_buf[slot] = tn(halves[...], grads[i])
        down_buf[slot] = tn(actives[i], result_grads[...])
        for copy in stores(i):
            copy.start()

    half = pl.ds(pl.multiple_of(dp[0] * 512, 512), 512)
    first = [
        begin(packed_hbm, packed, one_sem.at[0]),
        begin(own_hbm.at[:, half], halves.at[top], one_sem.at[1]),
        begin(grad_own_hbm, result_grads.at[top], one_sem.at[2]),
    ]
    fetch(0)
    finish(first)
    fetch(1)
    unpack(packed, [other, grad_other])
    halves[384:] = jnp.where(dp[0] == 0, other[:, :512], other[:, 512:])
    result_grads[384:] = grad_other[...]
    finish(loads(0))
    layer(0)

    def body(i, _):
        finish(loads(i))

        @pl.when(i < 7)
        def _():
            fetch(i + 1)

        @pl.when(i > 2)
        def _():
            finish(stores(i - 3))

        layer(i)
        products(i - 1)
        return 0

    lax.fori_loop(1, 8, body, 0)
    finish(stores(5))
    products(7)
    finish(stores(6))
    finish(stores(7))


def weights(*args):
    return call(
        weights_kernel, "weights", [WORD] + [HBM] * 7, [HBM, HBM],
        [arr(F32, 512, 4096), arr(F32, 2048, 1024)],
        [
            room(BF16, 3072, 256), room(BF16, 384, 1024), room(BF16, 384, 1024),
            room(BF16, 768, 512), room(BF16, 768, 1024), room(BF16, 8, 768, 512),
            room(BF16, 8, 768, 256), room(BF16, 8, 1024, 512), room(BF16, 8, 512, 1024),
            room(F32, 2, 512, 512), room(F32, 2, 256, 1024), sems(3),
            pltpu.SemaphoreType.DMA((8, 7)), pltpu.SemaphoreType.DMA((8, 3)),
        ],
        13, 46,
    )(*args)


def backward_kernel(
    spot, ints_hbm, gain2_hbm, back_hbm, cot_hbm, resid_hbm, wo_hbm, qkv_hbm,
    gain_out, bias_out, resid_grad_out, grads_out, keep_x, keep_z, send_x, send_z,
    ints, gain2, sums, packed, back, cot, resid, wo, qkv, resid_grad, branch, grads, in_sem, out_sem,
):
    load_packed = begin(back_hbm, packed, in_sem.at[0])
    smalls = [begin(ints_hbm[n], ints[n], in_sem.at[11 + n]) for n in range(4)]
    smalls.append(begin(gain2_hbm, gain2, in_sem.at[15]))
    seg_row, pad_row, expert_ids, slots = ints
    firsts = [begin(resid_hbm, resid, in_sem.at[1]), begin(cot_hbm, cot, in_sem.at[2])]
    groups = [((1 - spot[0] + i // 2) % 2) * 2 + i % 2 for i in range(4)]
    loads = []

    def fetch(i):
        if i < 4:
            rows = pl.ds(pl.multiple_of(groups[i] * 256, 256), 256)
            loads.append(
                [
                    begin(wo_hbm.at[rows], wo.at[i], in_sem.at[3 + 2 * i]),
                    begin(qkv_hbm.at[groups[i]], qkv.at[i], in_sem.at[4 + 2 * i]),
                ]
            )

    finish(smalls)
    dispatch = slot_rows(expert_ids[...], slots[...])
    bias = mask_bias(seg_row[...], pad_row[...])
    load_packed.wait()
    fetch(0)
    unpack_one(packed, back, 0)
    second_grad = tn(dispatch, back[...])
    finish(firsts)
    fetch(1)
    normal, factor = layer_stats(resid[...])
    sums[0][...] = jnp.sum(second_grad * normal, 0, keepdims=True)
    sums[1][...] = jnp.sum(second_grad, 0, keepdims=True)
    grad = cot[...].astype(F32) + norm_back(second_grad, normal, factor, gain2[...])
    resid_grad[...] = grad
    branch[...] = grad.astype(BF16)
    stores = [
        begin(resid_grad, resid_grad_out, out_sem.at[4, 0]),
        begin(sums[0], gain_out, out_sem.at[4, 1]),
        begin(sums[1], bias_out, out_sem.at[4, 2]),
    ]
    for i in range(4):
        finish(loads[i])
        fetch(i + 2)
        mixed_grad = nt(branch[...], wo[i]).astype(BF16)
        k = qkv[i, :, 256:512]
        q_heads = by_head(qkv[i, :, :256])
        grad_heads = by_head(mixed_grad)
        attention = softmax(q_heads, k, bias)
        pulled = nt(grad_heads, qkv[i, :, 512:])
        inner = jnp.sum(attention * pulled, -1, keepdims=True)
        score_grad = (attention * (pulled - inner)).astype(BF16)
        dq = nn(side_by_side(score_grad), by_head(k))
        dk = tn(score_grad, q_heads)
        dv = tn(attention.astype(BF16), grad_heads)
        grads[i, 0] = (dq * SCALE).astype(BF16)
        grads[i, 1] = (dk * SCALE).astype(BF16)
        grads[i, 2] = dv.astype(BF16)
        grads[i, 3] = branch[:, pl.ds(pl.multiple_of(groups[i] * 256, 256), 256)]
        stores.append(begin(grads.at[i, pl.ds(0, 3)], grads_out.at[i], out_sem.at[i, 4]))
        cols = pl.ds(256 * (i % 2), 256)
        pair_x, pair_z = (send_x, send_z) if i < 2 else (keep_x, keep_z)
        for mine in range(2):
            tensor_x = spot[1] if mine else 1 - spot[1]
            tensor_z = 2 + (spot[2] if mine else 1 - spot[2])
            stores.append(begin(grads.at[i, tensor_x], pair_x[mine].at[:, cols], out_sem.at[i, mine]))
            stores.append(begin(grads.at[i, tensor_z], pair_z[mine].at[:, cols], out_sem.at[i, 2 + mine]))
    finish(stores)


def backward(*args):
    pair = [arr(BF16, 256, 512)] * 2
    return call(
        backward_kernel, "backward",
        [WORD, [HBM] * 4] + [HBM] * 6,
        [HBM] * 4 + [[HBM, HBM]] * 4,
        [arr(F32, 1, 1024), arr(F32, 1, 1024), arr(F32, 256, 1024)]
        + [arr(BF16, 4, 3, 256, 256), pair, pair, pair, pair],
        [
            [room(jnp.int32, 1, 256)] * 4, room(F32, 1, 1024), [room(F32, 1, 1024)] * 2,
            room(BF16, 3072, 256), room(BF16, 384, 1024),
            room(BF16, 256, 1024), room(F32, 256, 1024),
            room(BF16, 4, 256, 1024), room(BF16, 4, 256, 768), room(F32, 256, 1024),
            room(BF16, 256, 1024), room(BF16, 4, 4, 256, 256), sems(16),
            pltpu.SemaphoreType.DMA((5, 5)),
        ],
        5, 10, 127,
    )(*args)


def combine_kernel(expert_ids, slots, message, resid, out, rows):
    unpack_one(message, rows, 1)
    dispatch = slot_rows(expert_ids[...], slots[...])
    out[...] = (resid[...] + tn(dispatch, rows[...])).astype(BF16)


def combine(*args):
    return call(
        combine_kernel, "combine",
        [whole(1, 256), whole(1, 256), whole(3072, 256), whole(256, 1024)],
        whole(256, 1024), arr(BF16, 256, 1024), [room(BF16, 384, 1024)], 0.5, 3,
    )(*args)


def input_kernel(
    spot, gain1_hbm, grads_hbm, qkv_hbm, tok_hbm, resid_grad_hbm, gain_out, bias_out, out_hbm,
    gain1, sums, out, grads, w_qkv, tok, resid_grad, sem,
):
    loads = []
    for i in range(4):
        col = ((1 - spot[0] + i // 2) % 2) * 512 + i % 2 * 256
        loads.append([])
        for n in range(3):
            here = grads.at[i, :, pl.ds(256 * n, 256)]
            loads[i].append(begin(grads_hbm.at[i, n], here, sem.at[6 * i + n + 3]))
            cols = pl.ds(pl.multiple_of(1024 * n + col, 256), 256)
            part = w_qkv.at[i, :, pl.ds(256 * n, 256)]
            loads[i].append(begin(qkv_hbm.at[:, cols], part, sem.at[6 * i + n]))
    lasts = [begin(gain1_hbm, gain1, sem.at[26]), begin(tok_hbm, tok, sem.at[24]), begin(resid_grad_hbm, resid_grad, sem.at[25])]
    grad = jnp.zeros((256, 1024), F32)
    for i in range(4):
        finish(loads[i])
        grad = grad + nt(grads[i], w_qkv[i])
    finish(lasts)
    normal, factor = layer_stats(tok[...].astype(F32))
    sums[0][...] = jnp.sum(grad * normal, 0, keepdims=True)
    sums[1][...] = jnp.sum(grad, 0, keepdims=True)
    out[...] = resid_grad[...] + norm_back(grad, normal, factor, gain1[...])
    stores = [
        begin(out, out_hbm, sem.at[27]),
        begin(sums[0], gain_out, sem.at[28]),
        begin(sums[1], bias_out, sem.at[29]),
    ]
    finish(stores)


def input_gradient(*args):
    return call(
        input_kernel, "input_gradient", [WORD] + [HBM] * 5, [HBM] * 3,
        [arr(F32, 1, 1024), arr(F32, 1, 1024), arr(F32, 256, 1024)],
        [
            room(F32, 1, 1024), [room(F32, 1, 1024)] * 2, room(F32, 256, 1024),
            room(BF16, 4, 256, 768), room(BF16, 4, 1024, 768), room(BF16, 256, 1024),
            room(F32, 256, 1024), sems(30),
        ],
        1.6, 10, 127,
    )(*args)


def partial_kernel(
    lines_hbm, acts_hbm, grads_hbm, out, lines, acts, grads, sums, small, in_sem, out_sem
):
    loads = []

    def fetch(n):
        if n < 8:
            rows = pl.ds(256 * (n % 4), 256)
            load = begin(acts_hbm[n], acts.at[n // 4, rows], in_sem.at[n])
            loads.append([load, begin(grads_hbm[n], grads.at[n // 4, rows], in_sem.at[8 + n])])

    for n in range(4):
        fetch(n)
    finish([begin(lines_hbm[n], lines[n], in_sem.at[16 + n]) for n in range(4)])
    rows = [line[...] for line in lines] + [jnp.zeros((124, 1024), F32)]
    small[...] = jnp.concatenate(rows, 0).T.astype(BF16)
    stores = [begin(small, out.at[:, pl.ds(1024, 128)], out_sem.at[2])]
    for j in range(2):
        total = jnp.zeros((1024, 512), F32)
        for half in range(2):
            first = 4 * j + 2 * half
            for n in (first, first + 1):
                finish(loads[n])
            fetch(first + 4)
            fetch(first + 5)
            rows = slice(512 * half, 512 * half + 512)
            total = total + tn(acts[j, rows], grads[j, rows])
        sums[j] = total.astype(BF16)
        stores.append(begin(sums.at[j], out.at[:, pl.ds(512 * j, 512)], out_sem.at[j]))
    finish(stores)


def partial_sums(*args):
    return call(
        partial_kernel, "partial_sums", [[HBM] * 4, [HBM] * 8, [HBM] * 8], HBM,
        arr(BF16, 1024, 1152),
        [
            [room(F32, 1, 1024)] * 4, room(BF16, 2, 1024, 1024), room(BF16, 2, 1024, 512), room(BF16, 2, 1024, 512),
            room(BF16, 1024, 128), sems(20), sems(3),
        ],
        2.2, 8, 127,
    )(*args)


def total_kernel(got_hbm, qkv_out, out_out, gain1, bias1, gain2, bias2, got, sem):
    loads = [begin(got_hbm.at[pl.ds(16 * i, 16)], got.at[i], sem.at[i]) for i in range(8)]
    totals = [jnp.zeros((8, 512), F32) for _ in range(8)]
    small = jnp.zeros((8, 128), F32)
    for i in range(8):
        loads[i].wait()
        for n in range(16):
            half = n % 2
            tensor_x = i % 2
            tensor_z = 2 + n // 4 % 2
            rows = got[i, n].astype(F32)
            totals[2 * tensor_x + half] = totals[2 * tensor_x + half] + rows[:, :512]
            totals[2 * tensor_z + half] = totals[2 * tensor_z + half] + rows[:, 512:1024]
            small = small + rows[:, 1024:]
    small = small.T
    for n, line in enumerate((gain1, bias1, gain2, bias2)):
        line[...] = small[n : n + 1, :]
    for tensor in range(4):
        target, start = (qkv_out, 1024 * tensor) if tensor < 3 else (out_out, 0)
        for half in range(2):
            first = start + 512 * half
            target[:, first : first + 512] = totals[2 * tensor + half]


def total_sums(got):
    return call(
        total_kernel, "total_sums", [HBM], [whole(8, 3072), whole(8, 1024)] + [whole(1, 8)] * 4,
        [arr(F32, 8, 3072), arr(F32, 8, 1024)] + [arr(F32, 1, 8)] * 4,
        [room(BF16, 8, 16, 8, 1152), sems(8)], 0.01, 2, 127,
    )(got)


def swap_pair(rows, axis):
    return lax.ppermute(rows, axis, [(i, i ^ 1) for i in range(4)])


def swap_pair_across(rows, axis):
    return lax.ppermute(rows, (axis, "core"), [(i, i ^ 3) for i in range(8)])


def exchange(rows):
    got = lax.all_to_all(rows.reshape(64, -1, 256), PEERS, 0, 0, tiled=True)
    return got.reshape(-1, 256)


def swap_core(rows):
    return lax.ppermute(rows, "core", SWAP)


def swap_dp(rows):
    return lax.ppermute(rows, "dp", SWAP)


def tie(*arrays):
    return lax.optimization_barrier(arrays)


def shards(
    tokens,
    segment_ids,
    padding,
    expert_ids,
    slots,
    norm1_gain,
    norm1_bias,
    qkv_weight,
    out_weight,
    norm2_gain,
    norm2_bias,
    up_weight,
    down_weight,
    cotangent,
):
    dp = lax.axis_index("dp").reshape(1)
    core = lax.axis_index("core").reshape(1)
    up = up_weight[0]
    down = down_weight[0]
    gain1 = norm1_gain[None]
    bias1 = norm1_bias[None]
    gain2 = norm2_gain[None]
    bias2 = norm2_bias[None]
    ids = expert_ids[None]
    places = slots[None]

    ints = [segment_ids, padding, ids, places]
    lines = [gain1, bias1, gain2, bias2]
    normed, qkv, mixed, resid, send = forward(
        ints, lines, tokens, cotangent, qkv_weight, out_weight
    )
    odd_x = lax.axis_index("x") % 2
    odd_z = lax.axis_index("z") % 2
    own_z = jnp.where(odd_z == 1, mixed, normed)
    other_z = jnp.where(odd_z == 0, mixed, normed)
    arrived, normed, own_z, other_z = tie(exchange(send), normed, own_z, other_z)
    came = swap_dp(arrived)
    came_x = swap_pair(normed, "x")
    came_z = swap_pair(other_z, "z")
    own, grad_own, active, grads, back = expert(arrived, up, down)
    back, came_x, came_z = tie(back, came_x, came_z)
    acts = [normed, swap_core(normed), came_x, swap_core(came_x)]
    acts += [own_z, swap_core(own_z), came_z, swap_core(came_z)]
    spot = jnp.stack([core[0], odd_x, odd_z])
    back, came, *acts = tie(exchange(back), came, *acts)
    gain2_grad, bias2_grad, resid_grad, qkv_grads, keep_x, keep_z, send_x, send_z = backward(
        spot, ints, gain2, back, cotangent, resid, out_weight, qkv,
    )
    pieces = []
    for axis, keep, send in (("x", keep_x, send_x), ("z", keep_z, send_z)):
        pieces += [keep[1], swap_core(send[1])]
        pieces += [swap_pair(keep[0], axis), swap_pair_across(send[0], axis)]
    gain1_grad, bias1_grad, input_grad = input_gradient(
        spot, gain1, qkv_grads, qkv_weight, tokens, resid_grad
    )
    part = partial_sums([gain1_grad, bias1_grad, gain2_grad, bias2_grad], acts, pieces)
    got = lax.all_to_all(part.reshape(128, 8, 1152), SPLIT, 0, 0, tiled=True)

    came, back, _ = tie(came, back, part)
    output = combine(ids, places, back, resid)
    up_grad, down_grad = weights(dp, own, grad_own, came, active, grads, up, down)
    got, up_grad, down_grad, output = tie(got, up_grad, down_grad, output)
    qkv_grad, out_grad, *small = total_sums(got)
    return (
        output,
        input_grad,
        small[0][0],
        small[1][0],
        qkv_grad,
        out_grad,
        small[2][0],
        small[3][0],
        up_grad[None],
        down_grad[None],
    )


def solution(mesh):
    fine = Mesh(mesh.devices.reshape(SIZES), SPLIT)
    rows = P(SPLIT, None)
    flat = P(SPLIT)
    experts = P(PEERS, None, None)
    placed = (rows, rows, rows, flat, flat, P(), P(), P(), P(), P(), P(), experts, experts, rows)
    halves = P(PEERS, "dp", None)
    return jax.shard_map(
        shards,
        mesh=fine,
        in_specs=placed,
        out_specs=(rows, rows, flat, flat, rows, rows, flat, flat, halves, halves),
        check_vma=False,
    )
```

```python
import jax
import jax.numpy as jnp
from jax import lax
from jax.experimental import pallas as pl
from jax.experimental.pallas import tpu as pltpu
from jax.sharding import Mesh
from jax.sharding import PartitionSpec as P

HEAD_DIM = 64
SPLIT = ("dp", "x", "z", "yh", "core")
PEERS = ("x", "z", "yh", "core")
SIZES = (2, 4, 4, 2, 2)
SWAP = [(0, 1), (1, 0)]
F32 = jnp.float32
BF16 = jnp.bfloat16
MIB = 1 << 20
SCALE = HEAD_DIM ** (-0.5)
GELU = 0.7978845608028654
CUBE = 0.044715
HBM = pl.BlockSpec(memory_space=pl.ANY)
WORD = pl.BlockSpec(memory_space=pltpu.SMEM)


def mm(a, b, dims):
    return lax.dot_general(a, b, (dims, ((), ())), preferred_element_type=F32)


def nn(a, b):
    return mm(a, b, ((1,), (0,)))


def nt(a, b):
    return mm(a, b, ((1,), (1,)))


def tn(a, b):
    return mm(a, b, ((0,), (0,)))


def layer_stats(values):
    center = values - jnp.mean(values, -1, keepdims=True)
    spread = jnp.mean(center * center, -1, keepdims=True)
    factor = lax.rsqrt(spread + 1e-05)
    return (center * factor, factor)


def norm_back(grad_out, normal, factor, gain):
    grad_hat = grad_out * gain
    return factor * (
        grad_hat
        - jnp.mean(grad_hat, -1, keepdims=True)
        - normal * jnp.mean(grad_hat * normal, -1, keepdims=True)
    )


def gelu_pair(v):
    square = v * v
    half = 0.5 + 0.5 * jnp.tanh(v * (GELU + GELU * CUBE * square))
    slope = half + half * (1.0 - half) * (v * (2 * GELU + 6 * GELU * CUBE * square))
    return v * half, slope


def iota(shape, dim):
    return lax.broadcasted_iota(jnp.int32, shape, dim)


def arr(dtype, *dims):
    return jax.ShapeDtypeStruct(dims, dtype)


def room(dtype, *dims):
    return pltpu.VMEM(dims, dtype)


def sems(n):
    return pltpu.SemaphoreType.DMA((n,))


def whole(*dims):
    return pl.BlockSpec(dims, lambda: (0,) * len(dims))


def call(kernel, name, ins, outs, outs_shape, scratch, flops, mib, limit=127):
    return pl.pallas_call(
        kernel,
        name=name,
        in_specs=ins,
        out_specs=outs,
        scratch_shapes=scratch,
        out_shape=outs_shape,
        compiler_params=pltpu.CompilerParams(vmem_limit_bytes=limit * MIB // 2),
        cost_estimate=pl.CostEstimate(
            flops=int(flops * 1e9), bytes_accessed=mib * MIB, transcendentals=0
        ),
    )


def begin(src, dst, sem):
    copy = pltpu.make_async_copy(src, dst, sem)
    copy.start()
    return copy


def finish(copies):
    for copy in copies:
        copy.wait()


def message_row(stacked, kinds):
    quarter = (stacked * 683) >> 16
    rest = stacked - quarter * 96
    start = quarter * 6 * kinds
    if kinds == 2:
        kind = (rest * 1366) >> 16
        rest = rest - kind * 48
        start = start + kind * 6
    expert_of = (rest * 10923) >> 16
    return expert_of * 24 * kinds + start + (rest - expert_of * 6)


def pack(kinds, out, done=None):
    count = len(kinds)
    size = 96 // count
    order = (iota((384, 384), 0) == message_row(iota((384, 384), 1), count)).astype(BF16)
    for g in range(4 * count):
        rows = slice(size * g, size * g + size)
        parts = []
        for q in range(4):
            parts += [kind[rows, 256 * q : 256 * q + 256] for kind in kinds]
        out[384 * g : 384 * g + 384] = nn(order, jnp.concatenate(parts, 0)).astype(BF16)
        if done is not None:
            done(g, pl.ds(384 * g, 384))


def unpack(message, kinds):
    count = len(kinds)
    size = 96 // count
    order = (message_row(iota((384, 384), 0), count) == iota((384, 384), 1)).astype(BF16)
    for g in range(4 * count):
        rows = slice(size * g, size * g + size)
        stack = nn(order, message[384 * g : 384 * g + 384]).astype(BF16)
        for q in range(4):
            for n, kind in enumerate(kinds):
                first = 96 * q + size * n
                kind[rows, 256 * q : 256 * q + 256] = stack[first : first + size]


def unpack_one(message, rows, kind):
    row = iota((192, 384), 0)
    row = row + ((row * 1366) >> 16) * 48 + 48 * kind
    order = (message_row(row, 2) == iota((192, 384), 1)).astype(BF16)
    for g in range(8):
        stack = nn(order, message[384 * g : 384 * g + 384]).astype(BF16)
        for q in range(4):
            part = stack[48 * q : 48 * q + 48]
            rows[48 * g : 48 * g + 48, 256 * q : 256 * q + 256] = part


def mask_bias(seg_row, pad_row):
    query = iota((256, 256), 0)
    key = iota((256, 256), 1)
    seg_key = jnp.broadcast_to(seg_row.astype(F32), (256, 256))
    allowed = (seg_key.T == seg_key) & (query >= key) & ((pad_row == 1) | (query == key))
    return jnp.where(allowed, 0.0, -1000000000.0)


def slot_rows(expert_ids, slots):
    return (iota((384, 256), 0) == expert_ids * 6 + slots).astype(BF16)


def by_head(block):
    head = iota((256, 256), 1) >> 6
    return jnp.concatenate(
        [jnp.where(head == h, block, jnp.zeros_like(block)) for h in range(4)], 0
    )


def side_by_side(stack):
    return jnp.concatenate([stack[256 * h : 256 * h + 256] for h in range(4)], 1)


def softmax(q_heads, keys, bias):
    masked = (nt(q_heads, keys) * SCALE).reshape(4, 256, 256) + bias[None]
    expanded = jnp.exp(masked - jnp.max(masked, -1, keepdims=True))
    return (expanded * (1.0 / jnp.sum(expanded, -1, keepdims=True))).reshape(1024, 256)


def forward_kernel(
    ints_hbm, lines_hbm, tok_hbm, cot_hbm, qkv_hbm, wo_hbm,
    normed_out, qkv_out, mixed_out, resid_out, send_out,
    ints, lines, tok, cot, w_qkv, wo, normed, qkv, mixed, resid, send, in_sem, out_sem,
):
    def fetch(g):
        if g < 4:
            for n in range(3):
                source = qkv_hbm.at[:, pl.ds(1024 * n + 256 * g, 256)]
                target = w_qkv.at[g, :, pl.ds(256 * n, 256)]
                loads.append(begin(source, target, in_sem.at[1 + 3 * g + n]))
        if g == 4:
            loads.append(begin(wo_hbm, wo, in_sem.at[13]))
        if g == 5:
            loads.append(begin(cot_hbm, cot, in_sem.at[14]))

    loads = [begin(tok_hbm, tok, in_sem.at[0])]
    smalls = [begin(ints_hbm[n], ints[n], in_sem.at[15 + n]) for n in range(4)]
    smalls += [begin(lines_hbm[n], lines[n], in_sem.at[19 + n]) for n in range(4)]
    seg_row, pad_row, expert_ids, slots = ints
    gain1, bias1, gain2, bias2 = lines
    fetch(0)
    fetch(1)
    finish(smalls)
    bias = mask_bias(seg_row[...], pad_row[...])
    loads[0].wait()
    fetch(2)
    normal, _ = layer_stats(tok[...].astype(F32))
    normed[...] = (normal * gain1[...] + bias1[...]).astype(BF16)
    stores = [begin(normed, normed_out, out_sem.at[0])]

    def project(g):
        finish(loads[1 + 3 * g : 4 + 3 * g])
        fetch(g + 3)
        qkv[g] = nn(normed[...], w_qkv[g]).astype(BF16)
        stores.append(begin(qkv.at[g], qkv_out.at[g], out_sem.at[1 + g]))

    project(0)
    for g in range(4):
        if g < 3:
            project(g + 1)
        attention = softmax(by_head(qkv[g, :, :256]), qkv[g, :, 256:512], bias)
        attention = side_by_side(attention.astype(BF16))
        mixed[:, 256 * g : 256 * g + 256] = nn(attention, by_head(qkv[g, :, 512:])).astype(BF16)
    stores.append(begin(mixed, mixed_out, out_sem.at[5]))
    loads[13].wait()
    resid[...] = tok[...].astype(F32) + nn(mixed[...], wo[...])
    stores.append(begin(resid, resid_out, out_sem.at[6]))
    normal, _ = layer_stats(resid[...])
    second = (normal * gain2[...] + bias2[...]).astype(BF16)
    dispatch = slot_rows(expert_ids[...], slots[...])
    loads[14].wait()

    def store(g, rows):
        stores.append(begin(send.at[rows], send_out.at[rows], out_sem.at[7 + g]))

    pack([nn(dispatch, second).astype(BF16), nn(dispatch, cot[...]).astype(BF16)], send, store)
    finish(stores)


def forward(*args):
    return call(
        forward_kernel, "forward",
        [[HBM] * 4, [HBM] * 4] + [HBM] * 4,
        [HBM] * 5,
        [
            arr(BF16, 256, 1024), arr(BF16, 4, 256, 768), arr(BF16, 256, 1024),
            arr(F32, 256, 1024), arr(BF16, 3072, 256),
        ],
        [
            [room(jnp.int32, 1, 256)] * 4, [room(F32, 1, 1024)] * 4,
            room(BF16, 256, 1024), room(BF16, 256, 1024), room(BF16, 4, 1024, 768),
            room(BF16, 1024, 1024), room(BF16, 256, 1024), room(BF16, 4, 256, 768), room(BF16, 256, 1024),
            room(F32, 256, 1024), room(BF16, 3072, 256), sems(23), sems(15),
        ],
        4, 14,
    )(*args)


def expert_kernel(
    packed_hbm, up_hbm, down_hbm, rows_out, crows_out, active_out, grad_out, send_out,
    packed, rows, crows, up, down, hidden, active, grad, send, in_sem, out_sem, one_sem,
):
    def fetch_up(i):
        if i < 4:
            source = up_hbm.at[:, pl.ds(1024 * i, 1024)]
            load_up.append(begin(source, up.at[i], in_sem.at[i, 0]))

    def fetch_down(i):
        if i < 4:
            source = down_hbm.at[pl.ds(1024 * i, 1024)]
            load_down.append(begin(source, down.at[i], in_sem.at[i, 1]))

    load_up = []
    load_down = []
    load_rows = begin(packed_hbm, packed, one_sem.at[0])
    fetch_up(0)
    load_rows.wait()
    fetch_up(1)
    fetch_down(0)
    unpack(packed, [rows, crows])
    load_up[0].wait()
    hidden[0] = nn(rows[...], up[0])
    stores = [begin(rows, rows_out, one_sem.at[1]), begin(crows, crows_out, one_sem.at[2])]
    for i in range(4):
        load_down[i].wait()
        fetch_down(i + 1)
        if i < 3:
            load_up[i + 1].wait()
            fetch_up(i + 2)
            hidden[(i + 1) % 2] = nn(rows[...], up[i + 1])
        pulled = nt(crows[...], down[i])
        low, slope = gelu_pair(hidden[i % 2])
        active[i] = low.astype(BF16)
        grad[i] = (pulled * slope).astype(BF16)
        for n in range(2):
            cols = pl.ds(512 * n, 512)
            tile = 2 * i + n
            stores.append(begin(active.at[i, :, cols], active_out.at[tile], out_sem.at[tile, 0]))
            stores.append(begin(grad.at[i, :, cols], grad_out.at[tile], out_sem.at[tile, 1]))
    back = jnp.zeros((384, 1024), F32)
    result = jnp.zeros((384, 1024), F32)
    for i in range(4):
        back = back + nt(grad[i], up[i])
    for i in range(4):
        result = result + nn(active[i], down[i])

    def store(g, rows):
        stores.append(begin(send.at[rows], send_out.at[rows], one_sem.at[3 + g]))

    pack([back.astype(BF16), result.astype(BF16)], send, store)
    finish(stores)


def expert(packed, up, down):
    rows = arr(BF16, 384, 1024)
    wide = arr(BF16, 8, 384, 512)
    return call(
        expert_kernel, "expert", [HBM] * 3, [HBM] * 5,
        [rows, rows, wide, wide, arr(BF16, 3072, 256)],
        [
            room(BF16, 3072, 256), room(BF16, 384, 1024), room(BF16, 384, 1024),
            room(BF16, 4, 1024, 1024), room(BF16, 4, 1024, 1024), room(F32, 2, 384, 1024),
            room(BF16, 4, 384, 1024), room(BF16, 4, 384, 1024), room(BF16, 3072, 256),
            pltpu.SemaphoreType.DMA((4, 2)), pltpu.SemaphoreType.DMA((8, 2)), sems(11),
        ],
        11, 30,
    )(packed, up, down)


def weights_kernel(
    dp, own_hbm, grad_own_hbm, packed_hbm, active_hbm, grad_hbm, up_hbm, down_hbm,
    up_out, down_out,
    packed, other, grad_other, halves, result_grads, grads, actives, up, down, up_buf, down_buf,
    one_sem, in_sem, out_sem,
):
    left = pl.ds(0, 256)
    right = pl.ds(256, 256)
    top = pl.ds(0, 384)

    def mine(i):
        return pl.ds(pl.multiple_of(dp[0] * 2048 + 256 * i, 256), 256)

    def rest(i):
        return pl.ds(pl.multiple_of((1 - dp[0]) * 2048 + 256 * i, 256), 256)

    def loads(i):
        part = pl.ds(pl.multiple_of(i % 2 * 256, 256), 256)
        near = dp[0] * 4 + i // 2
        far = (1 - dp[0]) * 4 + i // 2
        pairs = [
            (up_hbm.at[:, mine(i)], up.at[i, :, left]),
            (up_hbm.at[:, rest(i)], up.at[i, :, right]),
            (down_hbm.at[mine(i)], down.at[i, left]),
            (down_hbm.at[rest(i)], down.at[i, right]),
            (grad_hbm.at[near, :, part], grads.at[i, top, left]),
            (grad_hbm.at[far, :, part], grads.at[i, top, right]),
            (active_hbm.at[near, :, part], actives.at[i, top]),
        ]
        return [
            pltpu.make_async_copy(source, target, in_sem.at[i, n])
            for n, (source, target) in enumerate(pairs)
        ]

    def stores(i):
        slot = i % 2
        below = pl.ds(pl.multiple_of(256 * i, 256), 256)
        pairs = [
            (up_buf.at[slot, :, left], up_out.at[:, mine(i)]),
            (up_buf.at[slot, :, right], up_out.at[:, rest(i)]),
            (down_buf.at[slot], down_out.at[below]),
        ]
        return [
            pltpu.make_async_copy(source, target, out_sem.at[i, n])
            for n, (source, target) in enumerate(pairs)
        ]

    def fetch(i):
        for copy in loads(i):
            copy.start()

    def layer(i):
        active, slope = gelu_pair(nn(other[...], up[i]))
        actives[i, 384:] = active[:, :256].astype(BF16)
        grads[i, 384:] = (nt(grad_other[...], down[i]) * slope).astype(BF16)

    def products(i):
        slot = i % 2
        up_buf[slot] = tn(halves[...], grads[i])
        down_buf[slot] = tn(actives[i], result_grads[...])
        for copy in stores(i):
            copy.start()

    half = pl.ds(pl.multiple_of(dp[0] * 512, 512), 512)
    first = [
        begin(packed_hbm, packed, one_sem.at[0]),
        begin(own_hbm.at[:, half], halves.at[top], one_sem.at[1]),
        begin(grad_own_hbm, result_grads.at[top], one_sem.at[2]),
    ]
    fetch(0)
    finish(first)
    fetch(1)
    unpack(packed, [other, grad_other])
    halves[384:] = jnp.where(dp[0] == 0, other[:, :512], other[:, 512:])
    result_grads[384:] = grad_other[...]
    finish(loads(0))
    layer(0)

    def body(i, _):
        finish(loads(i))

        @pl.when(i < 7)
        def _():
            fetch(i + 1)

        @pl.when(i > 2)
        def _():
            finish(stores(i - 3))

        layer(i)
        products(i - 1)
        return 0

    lax.fori_loop(1, 8, body, 0)
    finish(stores(5))
    products(7)
    finish(stores(6))
    finish(stores(7))


def weights(*args):
    return call(
        weights_kernel, "weights", [WORD] + [HBM] * 7, [HBM, HBM],
        [arr(F32, 512, 4096), arr(F32, 2048, 1024)],
        [
            room(BF16, 3072, 256), room(BF16, 384, 1024), room(BF16, 384, 1024),
            room(BF16, 768, 512), room(BF16, 768, 1024), room(BF16, 8, 768, 512),
            room(BF16, 8, 768, 256), room(BF16, 8, 1024, 512), room(BF16, 8, 512, 1024),
            room(F32, 2, 512, 512), room(F32, 2, 256, 1024), sems(3),
            pltpu.SemaphoreType.DMA((8, 7)), pltpu.SemaphoreType.DMA((8, 3)),
        ],
        13, 46,
    )(*args)


def backward_kernel(
    spot, ints_hbm, gain2_hbm, back_hbm, cot_hbm, resid_hbm, wo_hbm, qkv_hbm,
    gain_out, bias_out, resid_grad_out, grads_out, keep_x, keep_z, send_x, send_z, send_near,
    ints, gain2, sums, packed, back, cot, resid, wo, qkv, resid_grad, branch, grads, in_sem, out_sem,
):
    load_packed = begin(back_hbm, packed, in_sem.at[0])
    smalls = [begin(ints_hbm[n], ints[n], in_sem.at[11 + n]) for n in range(4)]
    smalls.append(begin(gain2_hbm, gain2, in_sem.at[15]))
    seg_row, pad_row, expert_ids, slots = ints
    firsts = [begin(resid_hbm, resid, in_sem.at[1]), begin(cot_hbm, cot, in_sem.at[2])]
    groups = [((1 - spot[0] + i // 2) % 2) * 2 + i % 2 for i in range(4)]
    loads = []

    def fetch(i):
        if i < 4:
            rows = pl.ds(pl.multiple_of(groups[i] * 256, 256), 256)
            loads.append(
                [
                    begin(wo_hbm.at[rows], wo.at[i], in_sem.at[3 + 2 * i]),
                    begin(qkv_hbm.at[groups[i]], qkv.at[i], in_sem.at[4 + 2 * i]),
                ]
            )

    finish(smalls)
    dispatch = slot_rows(expert_ids[...], slots[...])
    bias = mask_bias(seg_row[...], pad_row[...])
    load_packed.wait()
    fetch(0)
    unpack_one(packed, back, 0)
    second_grad = tn(dispatch, back[...])
    finish(firsts)
    fetch(1)
    normal, factor = layer_stats(resid[...])
    sums[0][...] = jnp.sum(second_grad * normal, 0, keepdims=True)
    sums[1][...] = jnp.sum(second_grad, 0, keepdims=True)
    grad = cot[...].astype(F32) + norm_back(second_grad, normal, factor, gain2[...])
    resid_grad[...] = grad
    branch[...] = grad.astype(BF16)
    stores = [
        begin(resid_grad, resid_grad_out, out_sem.at[4, 0]),
        begin(sums[0], gain_out, out_sem.at[4, 1]),
        begin(sums[1], bias_out, out_sem.at[4, 2]),
    ]
    for i in range(4):
        finish(loads[i])
        fetch(i + 2)
        mixed_grad = nt(branch[...], wo[i]).astype(BF16)
        k = qkv[i, :, 256:512]
        q_heads = by_head(qkv[i, :, :256])
        grad_heads = by_head(mixed_grad)
        attention = softmax(q_heads, k, bias)
        pulled = nt(grad_heads, qkv[i, :, 512:])
        inner = jnp.sum(attention * pulled, -1, keepdims=True)
        score_grad = (attention * (pulled - inner)).astype(BF16)
        dq = nn(side_by_side(score_grad), by_head(k))
        dk = tn(score_grad, q_heads)
        dv = tn(attention.astype(BF16), grad_heads)
        grads[i, 0] = (dq * SCALE).astype(BF16)
        grads[i, 1] = (dk * SCALE).astype(BF16)
        grads[i, 2] = dv.astype(BF16)
        grads[i, 3] = branch[:, pl.ds(pl.multiple_of(groups[i] * 256, 256), 256)]
        stores.append(begin(grads.at[i, pl.ds(0, 3)], grads_out.at[i], out_sem.at[i, 4]))
        cols = pl.ds(256 * (i % 2), 256)
        if i < 2:
            pair_x, pair_z = (send_x, send_near.at[0]), (send_z, send_near.at[1])
        else:
            pair_x, pair_z = keep_x, keep_z
        for mine in range(2):
            tensor_x = spot[1] if mine else 1 - spot[1]
            tensor_z = 2 + (spot[2] if mine else 1 - spot[2])
            stores.append(begin(grads.at[i, tensor_x], pair_x[mine].at[:, cols], out_sem.at[i, mine]))
            stores.append(begin(grads.at[i, tensor_z], pair_z[mine].at[:, cols], out_sem.at[i, 2 + mine]))
    finish(stores)


def backward(*args):
    pair = [arr(BF16, 256, 512)] * 2
    return call(
        backward_kernel, "backward",
        [WORD, [HBM] * 4] + [HBM] * 6,
        [HBM] * 4 + [[HBM, HBM]] * 2 + [HBM] * 3,
        [arr(F32, 1, 1024), arr(F32, 1, 1024), arr(F32, 256, 1024)]
        + [arr(BF16, 4, 3, 256, 256), pair, pair] + pair + [arr(BF16, 2, 256, 512)],
        [
            [room(jnp.int32, 1, 256)] * 4, room(F32, 1, 1024), [room(F32, 1, 1024)] * 2,
            room(BF16, 3072, 256), room(BF16, 384, 1024),
            room(BF16, 256, 1024), room(F32, 256, 1024),
            room(BF16, 4, 256, 1024), room(BF16, 4, 256, 768), room(F32, 256, 1024),
            room(BF16, 256, 1024), room(BF16, 4, 4, 256, 256), sems(16),
            pltpu.SemaphoreType.DMA((5, 5)),
        ],
        5, 10, 127,
    )(*args)


def combine_kernel(expert_ids, slots, message, resid, out, rows):
    unpack_one(message, rows, 1)
    dispatch = slot_rows(expert_ids[...], slots[...])
    out[...] = (resid[...] + tn(dispatch, rows[...])).astype(BF16)


def combine(*args):
    return call(
        combine_kernel, "combine",
        [whole(1, 256), whole(1, 256), whole(3072, 256), whole(256, 1024)],
        whole(256, 1024), arr(BF16, 256, 1024), [room(BF16, 384, 1024)], 0.5, 3,
    )(*args)


def input_kernel(
    spot, gain1_hbm, grads_hbm, qkv_hbm, tok_hbm, resid_grad_hbm, gain_out, bias_out, out_hbm,
    gain1, sums, out, grads, w_qkv, tok, resid_grad, sem,
):
    loads = []
    for i in range(4):
        col = ((1 - spot[0] + i // 2) % 2) * 512 + i % 2 * 256
        loads.append([])
        for n in range(3):
            here = grads.at[i, :, pl.ds(256 * n, 256)]
            loads[i].append(begin(grads_hbm.at[i, n], here, sem.at[6 * i + n + 3]))
            cols = pl.ds(pl.multiple_of(1024 * n + col, 256), 256)
            part = w_qkv.at[i, :, pl.ds(256 * n, 256)]
            loads[i].append(begin(qkv_hbm.at[:, cols], part, sem.at[6 * i + n]))
    lasts = [begin(gain1_hbm, gain1, sem.at[26]), begin(tok_hbm, tok, sem.at[24]), begin(resid_grad_hbm, resid_grad, sem.at[25])]
    grad = jnp.zeros((256, 1024), F32)
    for i in range(4):
        finish(loads[i])
        grad = grad + nt(grads[i], w_qkv[i])
    finish(lasts)
    normal, factor = layer_stats(tok[...].astype(F32))
    sums[0][...] = jnp.sum(grad * normal, 0, keepdims=True)
    sums[1][...] = jnp.sum(grad, 0, keepdims=True)
    out[...] = resid_grad[...] + norm_back(grad, normal, factor, gain1[...])
    stores = [
        begin(out, out_hbm, sem.at[27]),
        begin(sums[0], gain_out, sem.at[28]),
        begin(sums[1], bias_out, sem.at[29]),
    ]
    finish(stores)


def input_gradient(*args):
    return call(
        input_kernel, "input_gradient", [WORD] + [HBM] * 5, [HBM] * 3,
        [arr(F32, 1, 1024), arr(F32, 1, 1024), arr(F32, 256, 1024)],
        [
            room(F32, 1, 1024), [room(F32, 1, 1024)] * 2, room(F32, 256, 1024),
            room(BF16, 4, 256, 768), room(BF16, 4, 1024, 768), room(BF16, 256, 1024),
            room(F32, 256, 1024), sems(30),
        ],
        1.6, 10, 127,
    )(*args)


def near_kernel(acts_hbm, grads_hbm, out, acts, grads, sums, in_sem, out_sem):
    loads = []
    for n in range(4):
        rows = pl.ds(256 * (n % 2), 256)
        load = begin(acts_hbm[n], acts.at[n // 2, rows], in_sem.at[n])
        source = grads_hbm[2].at[n // 2] if n % 2 else grads_hbm[n // 2]
        loads.append([load, begin(source, grads.at[n // 2, rows], in_sem.at[4 + n])])
    stores = []
    for j in range(2):
        finish(loads[2 * j] + loads[2 * j + 1])
        sums[j] = tn(acts[j], grads[j]).astype(BF16)
        stores.append(begin(sums.at[j], out.at[:, pl.ds(512 * j, 512)], out_sem.at[j]))
    finish(stores)


def near_sums(*args):
    return call(
        near_kernel, "near_sums", [[HBM] * 4, [HBM] * 3], HBM, arr(BF16, 1024, 1024),
        [
            room(BF16, 2, 512, 1024), room(BF16, 2, 512, 512), room(BF16, 2, 1024, 512),
            sems(8), sems(2),
        ],
        1.1, 5, 127,
    )(*args)


def partial_kernel(
    lines_hbm, acts_hbm, grads_hbm, near_hbm, out,
    lines, acts, grads, near, sums, small, in_sem, out_sem,
):
    loads = []
    for n in range(4):
        rows = pl.ds(256 * (n % 2), 256)
        load = begin(acts_hbm[n], acts.at[n // 2, rows], in_sem.at[n])
        loads.append([load, begin(grads_hbm[n], grads.at[n // 2, rows], in_sem.at[4 + n])])
    bases = [
        begin(near_hbm.at[:, pl.ds(512 * j, 512)], near.at[j], in_sem.at[8 + j]) for j in range(2)
    ]
    finish([begin(lines_hbm[n], lines[n], in_sem.at[10 + n]) for n in range(4)])
    rows = [line[...] for line in lines] + [jnp.zeros((124, 1024), F32)]
    small[...] = jnp.concatenate(rows, 0).T.astype(BF16)
    stores = [begin(small, out.at[:, pl.ds(1024, 128)], out_sem.at[2])]
    for j in range(2):
        finish(loads[2 * j] + loads[2 * j + 1])
        bases[j].wait()
        sums[j] = (near[j].astype(F32) + tn(acts[j], grads[j])).astype(BF16)
        stores.append(begin(sums.at[j], out.at[:, pl.ds(512 * j, 512)], out_sem.at[j]))
    finish(stores)


def partial_sums(*args):
    return call(
        partial_kernel, "partial_sums", [[HBM] * 4, [HBM] * 4, [HBM] * 4, HBM], HBM,
        arr(BF16, 1024, 1152),
        [
            [room(F32, 1, 1024)] * 4, room(BF16, 2, 512, 1024), room(BF16, 2, 512, 512),
            room(BF16, 2, 1024, 512), room(BF16, 2, 1024, 512), room(BF16, 1024, 128),
            sems(14), sems(3),
        ],
        1.1, 8, 127,
    )(*args)


def total_kernel(got_hbm, qkv_out, out_out, gain1, bias1, gain2, bias2, got, sem):
    loads = [begin(got_hbm.at[pl.ds(16 * i, 16)], got.at[i], sem.at[i]) for i in range(8)]
    totals = [jnp.zeros((8, 512), F32) for _ in range(8)]
    small = jnp.zeros((8, 128), F32)
    for i in range(8):
        loads[i].wait()
        for n in range(16):
            half = n % 2
            tensor_x = i % 2
            tensor_z = 2 + n // 4 % 2
            rows = got[i, n].astype(F32)
            totals[2 * tensor_x + half] = totals[2 * tensor_x + half] + rows[:, :512]
            totals[2 * tensor_z + half] = totals[2 * tensor_z + half] + rows[:, 512:1024]
            small = small + rows[:, 1024:]
    small = small.T
    for n, line in enumerate((gain1, bias1, gain2, bias2)):
        line[...] = small[n : n + 1, :]
    for tensor in range(4):
        target, start = (qkv_out, 1024 * tensor) if tensor < 3 else (out_out, 0)
        for half in range(2):
            first = start + 512 * half
            target[:, first : first + 512] = totals[2 * tensor + half]


def total_sums(got):
    return call(
        total_kernel, "total_sums", [HBM], [whole(8, 3072), whole(8, 1024)] + [whole(1, 8)] * 4,
        [arr(F32, 8, 3072), arr(F32, 8, 1024)] + [arr(F32, 1, 8)] * 4,
        [room(BF16, 8, 16, 8, 1152), sems(8)], 0.01, 2, 127,
    )(got)


def swap_pair(rows, axis):
    return lax.ppermute(rows, axis, [(i, i ^ 1) for i in range(4)])


def swap_pair_across(rows, axis):
    return lax.ppermute(rows, (axis, "core"), [(i, i ^ 3) for i in range(8)])


def exchange(rows):
    got = lax.all_to_all(rows.reshape(64, -1, 256), PEERS, 0, 0, tiled=True)
    return got.reshape(-1, 256)


def swap_core(rows):
    return lax.ppermute(rows, "core", SWAP)


def swap_dp(rows):
    return lax.ppermute(rows, "dp", SWAP)


def tie(*arrays):
    return lax.optimization_barrier(arrays)


def shards(
    tokens,
    segment_ids,
    padding,
    expert_ids,
    slots,
    norm1_gain,
    norm1_bias,
    qkv_weight,
    out_weight,
    norm2_gain,
    norm2_bias,
    up_weight,
    down_weight,
    cotangent,
):
    dp = lax.axis_index("dp").reshape(1)
    core = lax.axis_index("core").reshape(1)
    up = up_weight[0]
    down = down_weight[0]
    gain1 = norm1_gain[None]
    bias1 = norm1_bias[None]
    gain2 = norm2_gain[None]
    bias2 = norm2_bias[None]
    ids = expert_ids[None]
    places = slots[None]

    ints = [segment_ids, padding, ids, places]
    lines = [gain1, bias1, gain2, bias2]
    normed, qkv, mixed, resid, send = forward(
        ints, lines, tokens, cotangent, qkv_weight, out_weight
    )
    odd_x = lax.axis_index("x") % 2
    odd_z = lax.axis_index("z") % 2
    own_z = jnp.where(odd_z == 1, mixed, normed)
    other_z = jnp.where(odd_z == 0, mixed, normed)
    arrived, normed, own_z, other_z = tie(exchange(send), normed, own_z, other_z)
    came = swap_dp(arrived)
    came_x = swap_pair(normed, "x")
    came_z = swap_pair(other_z, "z")
    own, grad_own, active, grads, back = expert(arrived, up, down)
    back, came_x, came_z = tie(back, came_x, came_z)
    acts = [normed, swap_core(normed), came_x, swap_core(came_x)]
    acts += [own_z, swap_core(own_z), came_z, swap_core(came_z)]
    spot = jnp.stack([core[0], odd_x, odd_z])
    back, came, *acts = tie(exchange(back), came, *acts)
    gain2_grad, bias2_grad, resid_grad, qkv_grads, keep_x, keep_z, send_x, send_z, send_near = backward(
        spot, ints, gain2, back, cotangent, resid, out_weight, qkv,
    )
    near_grads = swap_core(send_near)
    far = []
    for axis, keep, send in (("x", keep_x, send_x), ("z", keep_z, send_z)):
        far += [swap_pair(keep[0], axis), swap_pair_across(send, axis)]
    gain1_grad, bias1_grad, input_grad = input_gradient(
        spot, gain1, qkv_grads, qkv_weight, tokens, resid_grad
    )
    near = near_sums(acts[:2] + acts[4:6], [keep_x[1], keep_z[1], near_grads])
    part = partial_sums(
        [gain1_grad, bias1_grad, gain2_grad, bias2_grad],
        acts[2:4] + acts[6:], far, near,
    )
    got = lax.all_to_all(part.reshape(128, 8, 1152), SPLIT, 0, 0, tiled=True)

    came, back, _ = tie(came, back, part)
    output = combine(ids, places, back, resid)
    up_grad, down_grad = weights(dp, own, grad_own, came, active, grads, up, down)
    got, up_grad, down_grad, output = tie(got, up_grad, down_grad, output)
    qkv_grad, out_grad, *small = total_sums(got)
    return (
        output,
        input_grad,
        small[0][0],
        small[1][0],
        qkv_grad,
        out_grad,
        small[2][0],
        small[3][0],
        up_grad[None],
        down_grad[None],
    )


def solution(mesh):
    fine = Mesh(mesh.devices.reshape(SIZES), SPLIT)
    rows = P(SPLIT, None)
    flat = P(SPLIT)
    experts = P(PEERS, None, None)
    placed = (rows, rows, rows, flat, flat, P(), P(), P(), P(), P(), P(), experts, experts, rows)
    halves = P(PEERS, "dp", None)
    return jax.shard_map(
        shards,
        mesh=fine,
        in_specs=placed,
        out_specs=(rows, rows, flat, flat, rows, rows, flat, flat, halves, halves),
        check_vma=False,
    )
```
